32 devices in a mesh: tok: 16 (over z, y, x), hid: 2 (over core).
Axes of the slice: x: 2, y: 2, z: 4, core: 2. Of those that a mesh axis runs over, the one named last changes fastest.
Arguments:
- tokens: bfloat16 [4096, 1536], P('tok', 'hid'), may hold values from -6 to 6
- ffn_gain: float32 [1536], replicated, may hold values from 0.5 to 1.5
- w_in: bfloat16 [1536, 6144], P('tok', 'hid'), may hold values from -0.15625 to 0.15625
- w_out: bfloat16 [6144, 1536], P('hid', 'tok'), may hold values from -0.078125 to 0.078125
- conv_gain: float32 [1536], replicated, may hold values from 0.5 to 1.5
- w_value: bfloat16 [1536, 1536], P(None, 'hid'), may hold values from -0.15625 to 0.15625
- w_gate: bfloat16 [1536, 1536], P(None, 'hid'), may hold values from -0.15625 to 0.15625
- depth_kernel: float32 [32, 1536], P(None, 'hid'), may hold values from -1 to 1
- bn_scale: float32 [1536], P('hid'), may hold values from 0.5 to 2
- bn_shift: float32 [1536], P('hid'), may hold values from -3 to 3
- w_proj: bfloat16 [1536, 1536], P(None, 'hid'), may hold values from -0.15625 to 0.15625
- lengths: int32 [64], replicated, may hold values from 1 to 128, 4096 in all
Outputs:
- layer_out: bfloat16 [4096, 1536], P('tok', 'hid')
The draws below stay inside these ranges and needn't reach their ends.
Inputs may be any that keep to these rules, and one draw needn't show every extreme that they name: The lengths sum to 4096 and the longest is exactly 128.
All inputs are finite; a program needn't handle non-finite values.
Results may differ from the reference program's by a relative error of at most 0.0095.
Values may be sent and summed in bfloat16 or wider, within the bound.
No kernel may reach another device: no remote copies, remote signals or barrier semaphores. Data moves between devices by JAX's collectives and lax.ppermute only.
A program may use at most 64 MiB of HBM per device.

```python
import math
import jax
import jax.numpy as jnp
import numpy as np
from jax import lax

D = 1536
FF = 6144
KERNEL = 32
UTTS = 64
TOK_DEV = 256
TOKENS = 4096
MOST = 128
N_TOK = 16


def block_scale(key, shape, shards, least, largest):
    def one(axis_at, parts):
        draws = jax.random.uniform(jax.random.fold_in(jax.random.fold_in(key, 6), axis_at), (parts,), jnp.float32, least / len(shards), largest / len(shards))
        return jnp.repeat(jnp.exp(draws), shape[axis_at] // parts).reshape((-1,) + (1,) * (len(shape) - axis_at - 1))

    factor_of = one(*shards[0])
    for cut in shards[1:]:
        factor_of = factor_of * one(*cut)
    return factor_of


def profile(amount, total, limit, skew):
    weights = [(1 << 20) // math.isqrt(rank ** skew) + 1 for rank in range(2, amount + 1)]
    rest, counts = total - limit - (amount - 1), [1] * (amount - 1)
    while rest > 0:
        free = [i for i in range(amount - 1) if counts[i] < limit]
        pool, left = sum([weights[i] for i in free]), rest
        for i in free:
            extra = min(limit - counts[i], max(1, left * weights[i] // pool), rest)
            counts[i] = counts[i] + extra
            rest = rest - extra
    return np.array([limit] + counts)


def ragged(own_key, count, total, limit, skew):
    if count == 2:
        one = jax.random.randint(own_key, (), max(1, total - limit), min(limit, total - 1) + 1)
        return jnp.stack([one, total - one])
    sizes = jnp.asarray(profile(count, total, limit, skew), jnp.int32)
    twos = (count - 1) // 2
    source_of, sink = sizes[1:1 + 2 * twos:2], sizes[2:2 + 2 * twos:2]
    margin = jnp.minimum(source_of - 1, limit - sink)
    shifted = jax.random.randint(jax.random.fold_in(own_key, 1), (twos,), 0, 1 << 20) % (margin + 1)
    sizes = sizes.at[1:1 + 2 * twos:2].set(source_of - shifted).at[2:2 + 2 * twos:2].set(sink + shifted)
    return sizes[jax.random.permutation(jax.random.fold_in(own_key, 2), count)]


def bell_draw(key, dims, scale, most, shards=(), held_as=jnp.bfloat16):
    array = scale * jax.random.normal(key, dims, jnp.float32)
    if shards:
        array = array * block_scale(key, dims, shards, -0.22, 0.18)
    return jnp.clip(array, -most, most).astype(held_as)


def setup_inputs(seed: int = 0) -> dict:
    seeds = jax.random.split(jax.random.key(seed), 13)
    tokens = bell_draw(seeds[0], (TOKENS, D), 1.0, 6.0, ((0, 16), (1, 2)))
    ffn_gain = jnp.clip(1.0 + 0.1 * jax.random.normal(seeds[1], (D,), jnp.float32), 0.5, 1.5)
    w_in = bell_draw(seeds[2], (D, FF), D ** -0.5, 0.15625, ((0, 16), (1, 2)))
    w_out = bell_draw(seeds[3], (FF, D), FF ** -0.5, 0.078125, ((0, 2), (1, 16)))
    conv_gain = jnp.clip(1.0 + 0.1 * jax.random.normal(seeds[4], (D,), jnp.float32), 0.5, 1.5)
    w_value = bell_draw(seeds[5], (D, D), D ** -0.5, 0.15625, ((1, 2),))
    w_gate = bell_draw(seeds[6], (D, D), D ** -0.5, 0.15625, ((1, 2),))
    depth_kernel = bell_draw(seeds[7], (KERNEL, D), KERNEL ** -0.5, 1.0, ((1, 2),), jnp.float32)
    bn_scale = jnp.clip(jnp.exp(math.log(2.0) - 1.3862944 * jax.random.uniform(seeds[8], (D,), jnp.float32) ** block_scale(seeds[8], (D,), ((0, 2),), -0.2, 0.2)), 0.5, 2.0)
    bn_shift = bell_draw(seeds[9], (D,), 0.5, 3.0, ((0, 2),), jnp.float32)
    w_proj = bell_draw(seeds[10], (D, D), D ** -0.5, 0.15625, ((1, 2),))
    lengths = ragged(seeds[11], UTTS, TOKENS, MOST, 2).astype(jnp.int32)
    return {"tokens": tokens, "ffn_gain": ffn_gain, "w_in": w_in, "w_out": w_out, "conv_gain": conv_gain, "w_value": w_value, "w_gate": w_gate, "depth_kernel": depth_kernel, "bn_scale": bn_scale, "bn_shift": bn_shift, "w_proj": w_proj, "lengths": lengths}


def norm_rows(values, gain):
    mean = lax.optimization_barrier(jnp.mean(values, axis=-1, keepdims=True))
    centred = values - mean
    var = lax.optimization_barrier(jnp.mean(centred * centred, axis=-1, keepdims=True))
    return centred * lax.rsqrt(var + 1e-05) * gain

def reference(tokens, ffn_gain, w_in, w_out, conv_gain, w_value, w_gate, depth_kernel, bn_scale, bn_shift, w_proj, lengths):
    blocks = tokens.reshape(N_TOK, TOK_DEV, D)

    def per_block(block):
        block_f = block.astype(jnp.float32)
        normed = norm_rows(block_f, ffn_gain).astype(jnp.bfloat16)
        hidden = jax.nn.silu(jnp.dot(normed, w_in, preferred_element_type=jnp.float32)).astype(jnp.bfloat16)
        ffn = jnp.dot(hidden, w_out, preferred_element_type=jnp.float32)
        mid = (block_f + 0.5 * ffn).astype(jnp.bfloat16)
        mid_normed = norm_rows(mid.astype(jnp.float32), conv_gain).astype(jnp.bfloat16)
        value = jnp.dot(mid_normed, w_value, preferred_element_type=jnp.float32)
        gate = jnp.dot(mid_normed, w_gate, preferred_element_type=jnp.float32)
        glu = (value * jax.nn.sigmoid(gate)).astype(jnp.bfloat16)
        return (mid, glu)
    mid, glu = lax.map(per_block, blocks)
    mid = mid.reshape(TOKENS, D)
    glu = glu.reshape(TOKENS, D).astype(jnp.float32)
    ends = jnp.cumsum(lengths).astype(jnp.int32)
    rows_all = jnp.arange(TOKENS, dtype=jnp.int32)
    utter = lax.optimization_barrier(jnp.sum((ends[None, :] <= rows_all[:, None]).astype(jnp.int32), axis=1))
    padded = jnp.pad(glu, ((15, 16), (0, 0)))
    utter_pad = jnp.pad(utter, (15, 16), constant_values=-1)
    conv = jnp.zeros((TOKENS, D), jnp.float32)
    for tap in range(KERNEL):
        same = (utter_pad[tap:tap + TOKENS] == utter)[:, None]
        conv = conv + jnp.where(same, padded[tap:tap + TOKENS] * depth_kernel[tap][None, :], 0.0)
    act = jax.nn.silu(conv * bn_scale + bn_shift).astype(jnp.bfloat16)
    projected = jnp.dot(act, w_proj, preferred_element_type=jnp.float32)
    return (mid.astype(jnp.float32) + projected).astype(jnp.bfloat16)
```

```python
import jax
import jax.numpy as jnp
from jax import lax
from jax.sharding import Mesh, PartitionSpec as P

SWAP = [(0, 1), (1, 0)]


def norm_rows(values, gain):
    mean = jnp.mean(values, axis=-1, keepdims=True)
    centred = values - mean
    var = jnp.mean(centred * centred, axis=-1, keepdims=True)
    return centred * lax.rsqrt(var + 1e-05) * gain


def padded(cells, axis, width):
    count = lax.axis_size(axis)
    ends = count - 1
    head = cells[:width]
    tail = cells[cells.shape[0] - width :]
    return jnp.concatenate(
        [
            lax.ppermute(tail, axis, [(i, (i + 1) % count) for i in range(ends)]),
            cells,
            lax.ppermute(head, axis, [((i + 1) % count, i) for i in range(ends)]),
        ],
        axis=0,
    )


def conv_module(mid_own, mid_full, axis, conv_gain, w_value, w_gate, depth_kernel, bn_scale, bn_shift, w_proj, lengths):
    rows, width = mid_own.shape
    mid_normed = norm_rows(mid_full.astype(jnp.float32), conv_gain).astype(jnp.bfloat16)
    value = jnp.dot(mid_normed, w_value, preferred_element_type=jnp.float32)
    gate = jnp.dot(mid_normed, w_gate, preferred_element_type=jnp.float32)
    glu = (value * jax.nn.sigmoid(gate)).astype(jnp.bfloat16)
    extended = padded(glu, axis, 16).astype(jnp.float32)
    ends = jnp.cumsum(lengths)
    first_row = lax.axis_index(axis) * rows - 16
    positions = first_row + jnp.arange(rows + 32, dtype=jnp.int32)
    utter = jnp.sum((ends[None, :] <= positions[:, None]).astype(jnp.int32), axis=1)
    centre = utter[16 : 16 + rows]
    conv = jnp.zeros((rows, width), jnp.float32)
    for tap in range(depth_kernel.shape[0]):
        same = (utter[tap + 1 : tap + 1 + rows] == centre)[:, None]
        conv = conv + jnp.where(
            same, extended[tap + 1 : tap + 1 + rows] * depth_kernel[tap][None, :], 0.0
        )
    act = jax.nn.silu(conv * bn_scale + bn_shift).astype(jnp.bfloat16)
    act_full = lax.all_gather(act, "hid", axis=1, tiled=True)
    projected = jnp.dot(act_full, w_proj, preferred_element_type=jnp.float32)
    return (mid_own.astype(jnp.float32) + projected).astype(jnp.bfloat16)


def gathered_ffn(tokens, ffn_gain, w_in, w_out):
    whole = lax.all_gather(tokens, "hid", axis=1, tiled=True)
    normed = norm_rows(whole.astype(jnp.float32), ffn_gain).astype(jnp.bfloat16)
    pre = jnp.dot(
        normed, lax.all_gather(w_in, "tok", axis=0, tiled=True), preferred_element_type=jnp.float32
    )
    hidden = jax.nn.silu(pre).astype(jnp.bfloat16)
    partial_sum = jnp.dot(
        hidden, lax.all_gather(w_out, "tok", axis=1, tiled=True), preferred_element_type=jnp.float32
    )
    share = lax.psum_scatter(
        partial_sum.astype(jnp.bfloat16), "hid", scatter_dimension=1, tiled=True
    ).astype(jnp.float32)
    mid_own = (tokens.astype(jnp.float32) + 0.5 * share).astype(jnp.bfloat16)
    return mid_own, lax.all_gather(mid_own, "hid", axis=1, tiled=True)


GROUP = ("bh", "bl")


def partner(values, step):
    return lax.ppermute(values, GROUP, [(i, i ^ step) for i in range(4)])


def ordered(first, second, index, axis):
    return jnp.where(
        index == 0, jnp.stack([first, second], axis), jnp.stack([second, first], axis)
    )


def grouped_ffn(tokens, ffn_gain, w_in, w_out):
    rows, width = tokens.shape
    half = rows // 2
    me_c = lax.axis_index("hid")
    me_a = lax.axis_index("ah")
    me_l = lax.axis_index("al")
    whole = lax.all_gather(tokens, "hid", axis=1, tiled=True)
    normed = norm_rows(whole.astype(jnp.float32), ffn_gain).astype(jnp.bfloat16)
    mine = lax.dynamic_slice_in_dim(normed, me_c * half, half, 0)
    x_own = jnp.concatenate([mine] + [partner(mine, k) for k in (1, 2, 3)], axis=0)
    x_oth = lax.ppermute(x_own, "hid", SWAP)
    x = jnp.concatenate([x_own, x_oth], axis=0)

    def recut(w):
        return lax.all_to_all(
            w.reshape(w.shape[0], 4, w.shape[1] // 4).transpose(1, 0, 2), GROUP, 0, 0
        )

    def spread(own):
        far = lax.ppermute(own, "ah", SWAP)
        own_l = lax.ppermute(own, "al", SWAP)
        far_l = lax.ppermute(far, "al", SWAP)
        def place(a, b):
            return ordered(a, b, me_l, 1).reshape(-1, own.shape[-1])
        return place(own, own_l), place(far, far_l)

    in_own, in_far = spread(recut(w_in))
    out_own, out_far = spread(recut(w_out.T))
    w_full = ordered(in_own, in_far, me_a, 0).reshape(-1, in_own.shape[-1])
    pre = jnp.dot(x, w_full, preferred_element_type=jnp.float32)
    hidden = jax.nn.silu(pre).astype(jnp.bfloat16)

    def sums(w):
        part = lax.dot_general(
            hidden, w, (((1,), (1,)), ((), ())), preferred_element_type=jnp.float32
        )
        kept, sent = part[: rows * 2], part[rows * 2 :]
        total = (
            kept + lax.ppermute(sent.astype(jnp.bfloat16), "hid", SWAP).astype(jnp.float32)
        ).astype(jnp.bfloat16)
        ffn = total[:half].astype(jnp.float32)
        for k in (1, 2, 3):
            ffn = ffn + partner(total[k * half : (k + 1) * half], k).astype(jnp.float32)
        return ffn

    ffn = ordered(sums(out_own), sums(out_far), me_a, 1).reshape(half, -1)
    mine_tok = lax.dynamic_slice_in_dim(whole, me_c * half, half, 0).astype(jnp.float32)
    mid_rows = (mine_tok + 0.5 * ffn).astype(jnp.bfloat16)
    mid_full = lax.all_gather(mid_rows, "hid", axis=0, tiled=True)
    mid_own = lax.dynamic_slice_in_dim(mid_full, me_c * width, width, 1)
    return mid_own, mid_full


def solution(mesh):
    n_tok, n_hid = mesh.shape["tok"], mesh.shape["hid"]
    grouped = n_tok == 16 and n_hid == 2
    if grouped:
        tok = ("ah", "bh", "bl", "al")
        inner = Mesh(mesh.devices.reshape(2, 2, 2, 2, n_hid), tok + ("hid",))
    else:
        tok, inner = "tok", mesh

    def local(tokens, ffn_gain, w_in, w_out, conv_gain, *rest):
        ffn = grouped_ffn if grouped else gathered_ffn
        mid_own, mid_full = ffn(tokens, ffn_gain, w_in, w_out)
        return conv_module(mid_own, mid_full, tok, conv_gain, *rest)

    placed = (
        P(tok, "hid"),
        P(),
        P(tok, "hid"),
        P("hid", tok),
        P(),
        P(None, "hid"),
        P(None, "hid"),
        P(None, "hid"),
        P("hid"),
        P("hid"),
        P(None, "hid"),
        P(),
    )
    return jax.shard_map(
        local, mesh=inner, in_specs=placed, out_specs=P(tok, "hid"), check_vma=False
    )
```

```python
import jax
import jax.numpy as jnp
from jax import lax
from jax.experimental import pallas as pl
from jax.experimental.pallas import tpu as pltpu
from jax.sharding import Mesh, PartitionSpec as P

SWAP = [(0, 1), (1, 0)]


def norm_rows(values, gain):
    mean = jnp.mean(values, axis=-1, keepdims=True)
    centred = values - mean
    var = jnp.mean(centred * centred, axis=-1, keepdims=True)
    return centred * lax.rsqrt(var + 1e-05) * gain


def padded(cells, axis, width):
    count = lax.axis_size(axis)
    ends = count - 1
    head = cells[:width]
    tail = cells[cells.shape[0] - width :]
    return jnp.concatenate(
        [
            lax.ppermute(tail, axis, [(i, (i + 1) % count) for i in range(ends)]),
            cells,
            lax.ppermute(head, axis, [((i + 1) % count, i) for i in range(ends)]),
        ],
        axis=0,
    )


def conv_module(mid_own, mid_full, axis, conv_gain, w_value, w_gate, depth_kernel, bn_scale, bn_shift, w_proj, lengths):
    rows, width = mid_own.shape
    mid_normed = norm_rows(mid_full.astype(jnp.float32), conv_gain).astype(jnp.bfloat16)
    value = jnp.dot(mid_normed, w_value, preferred_element_type=jnp.float32)
    gate = jnp.dot(mid_normed, w_gate, preferred_element_type=jnp.float32)
    glu = (value * jax.nn.sigmoid(gate)).astype(jnp.bfloat16)
    extended = padded(glu, axis, 16).astype(jnp.float32)
    ends = jnp.cumsum(lengths)
    first_row = lax.axis_index(axis) * rows - 16
    positions = first_row + jnp.arange(rows + 32, dtype=jnp.int32)
    utter = jnp.sum((ends[None, :] <= positions[:, None]).astype(jnp.int32), axis=1)
    centre = utter[16 : 16 + rows]
    conv = jnp.zeros((rows, width), jnp.float32)
    for tap in range(depth_kernel.shape[0]):
        same = (utter[tap + 1 : tap + 1 + rows] == centre)[:, None]
        conv = conv + jnp.where(
            same, extended[tap + 1 : tap + 1 + rows] * depth_kernel[tap][None, :], 0.0
        )
    act = jax.nn.silu(conv * bn_scale + bn_shift).astype(jnp.bfloat16)
    act_full = lax.all_gather(act, "hid", axis=1, tiled=True)
    projected = jnp.dot(act_full, w_proj, preferred_element_type=jnp.float32)
    return (mid_own.astype(jnp.float32) + projected).astype(jnp.bfloat16)


def gathered_ffn(tokens, ffn_gain, w_in, w_out):
    whole = lax.all_gather(tokens, "hid", axis=1, tiled=True)
    normed = norm_rows(whole.astype(jnp.float32), ffn_gain).astype(jnp.bfloat16)
    pre = jnp.dot(
        normed, lax.all_gather(w_in, "tok", axis=0, tiled=True), preferred_element_type=jnp.float32
    )
    hidden = jax.nn.silu(pre).astype(jnp.bfloat16)
    partial_sum = jnp.dot(
        hidden, lax.all_gather(w_out, "tok", axis=1, tiled=True), preferred_element_type=jnp.float32
    )
    share = lax.psum_scatter(
        partial_sum.astype(jnp.bfloat16), "hid", scatter_dimension=1, tiled=True
    ).astype(jnp.float32)
    mid_own = (tokens.astype(jnp.float32) + 0.5 * share).astype(jnp.bfloat16)
    return mid_own, lax.all_gather(mid_own, "hid", axis=1, tiled=True)


GROUP = ("bh", "bl")
VMEM_LIMIT = 40 * 2**20
VMEM = pl.BlockSpec(memory_space=pltpu.VMEM)
SMEM = pl.BlockSpec(memory_space=pltpu.SMEM)


def kernel_call(body, outs, ins, scratch=(), scalars=0):
    return pl.pallas_call(
        body,
        out_shape=[jax.ShapeDtypeStruct(shape, dtype) for shape, dtype in outs],
        in_specs=[SMEM] * scalars + [VMEM] * (len(ins) - scalars),
        out_specs=[VMEM] * len(outs),
        scratch_shapes=list(scratch),
        compiler_params=pltpu.CompilerParams(vmem_limit_bytes=VMEM_LIMIT),
        cost_estimate=pl.CostEstimate(flops=0, bytes_accessed=0, transcendentals=0),
    )(*ins)


def f32(values):
    return values.astype(jnp.float32)


def silu(values):
    return values / (1.0 + jnp.exp(-values))


def cut_kernel(in_ref, out_ref, in_cut_ref, out_cut_ref):
    parts, _, width = in_cut_ref.shape
    for part in range(parts):
        at = slice(part * width, (part + 1) * width)
        in_cut_ref[part] = in_ref[:, at]
        out_cut_ref[part] = out_ref[:, at]


def part_kernel(both_ref, first_ref, second_ref):
    half = first_ref.shape[0]
    first_ref[...] = both_ref[:half]
    second_ref[...] = both_ref[half:]


def norm_kernel(start_ref, whole_ref, gain_ref, mine_ref, out_ref):
    rows = mine_ref.shape[0]
    mine = whole_ref[pl.ds(pl.multiple_of(start_ref[0], rows), rows), :]
    mine_ref[...] = mine
    out_ref[...] = norm_rows(f32(mine), gain_ref[...]).astype(jnp.bfloat16)


def join_kernel(*refs):
    *pieces, out_ref = refs
    rows = pieces[0].shape[0]
    for i, piece in enumerate(pieces):
        out_ref[i * rows : (i + 1) * rows] = piece[...]


def interleave(full_ref, base, own_refs, other_refs, me_l):
    block = own_refs[0].shape[1]
    for refs, turn in ((own_refs, me_l), (other_refs, 1 - me_l)):
        blocks = [(ref, j) for ref in refs for j in range(ref.shape[0])]
        for i, (ref, j) in enumerate(blocks):
            at = pl.multiple_of(base + (2 * i + turn) * block, block)
            full_ref[pl.ds(at, block), :] = ref[j]


def hidden_kernel(me_ref, x_ref, o_ref, ox_ref, z_ref, zx_ref, h_ref, w_ref):
    me_l, me_a = me_ref[0], me_ref[2]
    part = w_ref.shape[0] // 2
    interleave(w_ref, me_a * part, [o_ref], [ox_ref], me_l)
    interleave(w_ref, (1 - me_a) * part, [z_ref], [zx_ref], me_l)
    step = 256
    for at in range(0, x_ref.shape[0], step):
        pre = jnp.dot(x_ref[at : at + step, :], w_ref[...], preferred_element_type=jnp.float32)
        h_ref[at : at + step, :] = silu(pre).astype(jnp.bfloat16)


def sums_kernel(me_ref, own_ref, oth_ref, first_ref, second_ref, *refs):
    *others, kept_ref, sent_ref, w_ref = refs
    interleave(w_ref, 0, [first_ref, second_ref], others, me_ref[0])
    step = 256
    for h_ref, out_ref in ((oth_ref, sent_ref), (own_ref, kept_ref)):
        for at in range(0, h_ref.shape[0], step):
            out_ref[at : at + step, :] = lax.dot_general(
                h_ref[at : at + step, :],
                w_ref[...],
                (((1,), (1,)), ((), ())),
                preferred_element_type=jnp.float32,
            ).astype(out_ref.dtype)


def add_kernel(kept_ref, came_ref, *out_refs):
    rows = out_refs[0].shape[0]
    for k, out_ref in enumerate(out_refs):
        at = slice(k * rows, (k + 1) * rows)
        out_ref[...] = (kept_ref[at, :] + f32(came_ref[at, :])).astype(out_ref.dtype)


def mid_kernel(me_ref, mine_ref, *refs):
    *sums, out_ref = refs
    for place, part in ((me_ref[2], sums[:4]), (1 - me_ref[2], sums[4:])):
        total = part[0][...]
        for other in part[1:]:
            total = total + f32(other[...])
        width = part[0].shape[1]
        at = pl.ds(pl.multiple_of(place * width, width), width)
        out_ref[:, at] = (f32(mine_ref[:, at]) + 0.5 * total).astype(jnp.bfloat16)


HALO = 16


def utter_kernel(first_ref, lengths_ref, out_ref):
    position = first_ref[0] + lax.broadcasted_iota(jnp.int32, out_ref.shape, 0)

    def step(u, carry):
        end, utter = carry
        end = end + lengths_ref[u]
        return end, utter + jnp.where(position >= end, 1, 0)

    zero = jnp.zeros(out_ref.shape, jnp.int32)
    out_ref[...] = lax.fori_loop(0, lengths_ref.shape[0], step, (jnp.int32(0), zero))[1]


def glu_kernel(mid_ref, gain_ref, value_ref, gate_ref, glu_ref, head_ref, tail_ref):
    normed = norm_rows(f32(mid_ref[...]), gain_ref[...]).astype(jnp.bfloat16)
    value = jnp.dot(normed, value_ref[...], preferred_element_type=jnp.float32)
    gate = jnp.dot(normed, gate_ref[...], preferred_element_type=jnp.float32)
    glu = (value / (1.0 + jnp.exp(-gate))).astype(jnp.bfloat16)
    glu_ref[...] = glu
    head_ref[...] = glu[:HALO]
    tail_ref[...] = glu[glu.shape[0] - HALO :]


def conv_rows(ext_ref, utter_ref, taps_ref, scale_ref, shift_ref, out_ref, ext_at, utter_at, out_at, rows):
    lanes = 128
    taps = taps_ref.shape[0]
    span = rows + taps - 8

    def column(j, _):
        at = pl.ds(pl.multiple_of(j * lanes, lanes), lanes)
        centre = utter_ref[utter_at + HALO : utter_at + HALO + rows, :]
        total = jnp.zeros((rows, lanes), jnp.float32)
        for r in range(8):
            cells = ext_ref[ext_at + 1 + r : ext_at + 1 + r + span, at]
            utter = utter_ref[utter_at + 1 + r : utter_at + 1 + r + span, :]
            for q in range(0, taps, 8):
                term = cells[q : q + rows] * taps_ref[q + r : q + r + 1, at]
                total = total + jnp.where(utter[q : q + rows] == centre, term, 0.0)
        act = silu(total * scale_ref[:, at] + shift_ref[:, at])
        out_ref[out_at : out_at + rows, at] = act.astype(out_ref.dtype)
        return 0

    lax.fori_loop(0, out_ref.shape[1] // lanes, column, 0)


def inner_conv_kernel(glu_ref, utter_ref, taps_ref, scale_ref, shift_ref, out_ref, ext_ref):
    ext_ref[...] = f32(glu_ref[...])
    step = 32
    for at in range(HALO, out_ref.shape[0] - HALO, step):
        conv_rows(
            ext_ref, utter_ref, taps_ref, scale_ref, shift_ref, out_ref, at - HALO, at, at, step
        )


def edge_conv_kernel(
    act_ref, top_ref, glu_ref, bottom_ref, utter_ref, taps_ref, scale_ref, shift_ref, out_ref, ext_ref
):
    rows = out_ref.shape[0]
    last = rows - HALO
    out_ref[HALO:last, :] = act_ref[HALO:last, :]
    ext_ref[:HALO, :] = f32(top_ref[...])
    ext_ref[HALO : 3 * HALO, :] = f32(glu_ref[: 2 * HALO, :])
    ext_ref[3 * HALO : 5 * HALO, :] = f32(glu_ref[rows - 2 * HALO :, :])
    ext_ref[5 * HALO :, :] = f32(bottom_ref[...])
    rest = (utter_ref, taps_ref, scale_ref, shift_ref, out_ref)
    conv_rows(ext_ref, *rest, 0, 0, 0, HALO)
    conv_rows(ext_ref, *rest, 3 * HALO, last, last, HALO)


def utterances(rows, axis, lengths):
    return kernel_call(
        utter_kernel,
        [((rows + 2 * HALO, 128), jnp.int32)],
        [(lax.axis_index(axis) * rows - HALO)[None], lengths],
        scalars=2,
    )[0]


def grouped_conv_module(
    mid_own, mid_full, axis, utter, conv_gain, w_value, w_gate, depth_kernel, bn_scale, bn_shift, w_proj
):
    rows, width = mid_own.shape
    bf16 = jnp.bfloat16
    glu, head, tail = kernel_call(
        glu_kernel,
        [((rows, width), bf16)] + [((HALO, width), bf16)] * 2,
        [mid_full, conv_gain[None, :], w_value, w_gate],
    )
    count = lax.axis_size(axis)
    top = lax.ppermute(tail, axis, [(i, i + 1) for i in range(count - 1)])
    bottom = lax.ppermute(head, axis, [(i + 1, i) for i in range(count - 1)])
    rest = [utter, depth_kernel, bn_scale[None, :], bn_shift[None, :]]
    (act,) = kernel_call(
        inner_conv_kernel,
        [((rows, width), bf16)],
        [glu, *rest],
        scratch=[pltpu.VMEM((rows, width), jnp.float32)],
    )
    (act,) = kernel_call(
        edge_conv_kernel,
        [((rows, width), bf16)],
        [act, top, glu, bottom, *rest],
        scratch=[pltpu.VMEM((6 * HALO, width), jnp.float32)],
    )
    act_full = lax.all_gather(act, "hid", axis=1, tiled=True)
    projected = jnp.dot(act_full, w_proj, preferred_element_type=jnp.float32)
    return (mid_own.astype(jnp.float32) + projected).astype(jnp.bfloat16)


def partner(values, step):
    return lax.ppermute(values, GROUP, [(i, i ^ step) for i in range(4)])


def swap(values, axis):
    return lax.ppermute(values, axis, SWAP)


def recut(parts):
    return lax.all_to_all(parts, GROUP, 0, 0)


def grouped_ffn(tokens, ffn_gain, w_in, w_out, early):
    rows, width = tokens.shape
    half = rows // 2
    shard, hid = w_in.shape
    wide = 2 * width
    units = hid // 4
    bf16 = jnp.bfloat16
    me_c = lax.axis_index("hid")
    me = jnp.stack([lax.axis_index("al"), me_c, lax.axis_index("ah")])
    tie = lax.optimization_barrier

    in_cut, out_cut = kernel_call(cut_kernel, [((4, shard, units), bf16)] * 2, [w_in, w_out.T])
    in_far = swap(in_cut, "ah")
    out_o = recut(out_cut)
    in_o = recut(in_cut)
    out_1, out_2 = kernel_call(part_kernel, [((2, shard, units), bf16)] * 2, [out_o])
    out_x1 = swap(out_1, "al")
    out_x2 = swap(out_2, "al")
    whole = lax.all_gather(tokens, "hid", axis=1, tiled=True)
    mine, normed = kernel_call(
        norm_kernel,
        [((half, wide), bf16)] * 2,
        [(me_c * half)[None], whole, ffn_gain[None, :]],
        scalars=1,
    )
    frames1 = partner(normed, 1)
    in_far, out_1, out_2, out_x1, out_x2, normed, frames1, early = tie(
        (in_far, out_1, out_2, out_x1, out_x2, normed, frames1, early)
    )
    out_z1 = swap(out_1, "ah")
    in_ox = swap(in_o, "al")
    in_z = recut(in_far)
    frames3 = partner(normed, 3)
    out_z1, in_ox, in_z, out_2, normed, frames3 = tie((out_z1, in_ox, in_z, out_2, normed, frames3))
    out_z2 = swap(out_2, "ah")
    in_zx = swap(in_z, "al")
    frames2 = partner(normed, 2)
    (x_own,) = kernel_call(
        join_kernel, [((4 * half, wide), bf16)], [normed, frames1, frames2, frames3]
    )
    out_z1, out_z2, in_zx, x_own = tie((out_z1, out_z2, in_zx, x_own))
    out_zx1 = swap(out_z1, "al")
    out_zx2 = swap(out_z2, "al")
    x_oth = swap(x_own, "hid")

    def units_of(x):
        return kernel_call(
            hidden_kernel,
            [((4 * half, units), bf16)],
            [me, x, in_o, in_ox, in_z, in_zx],
            scratch=[pltpu.VMEM((wide, units), bf16)],
            scalars=1,
        )[0]

    hidden = [units_of(x_own), units_of(x_oth)]

    def products(*blocks):
        return kernel_call(
            sums_kernel,
            [((4 * half, width), jnp.float32), ((4 * half, width), bf16)],
            [me, *hidden, *blocks],
            scratch=[pltpu.VMEM((width, units), bf16)],
            scalars=1,
        )

    def scatter(kept, sent):
        total = kernel_call(
            add_kernel,
            [((half, width), jnp.float32)] + [((half, width), bf16)] * 3,
            [kept, swap(sent, "hid")],
        )
        return [total[0]] + [partner(v, k + 1) for k, v in enumerate(total[1:])]

    near, out_zx1, out_zx2 = tie((products(out_1, out_2, out_x1, out_x2), out_zx1, out_zx2))
    far = products(out_z1, out_z2, out_zx1, out_zx2)
    (mid_rows,) = kernel_call(
        mid_kernel, [((half, wide), bf16)], [me, mine, *scatter(*near), *scatter(*far)], scalars=1
    )
    mid_full = lax.all_gather(mid_rows, "hid", axis=0, tiled=True)
    mid_own = lax.dynamic_slice_in_dim(mid_full, me_c * width, width, 1)
    return mid_own, mid_full, early


def solution(mesh):
    n_tok, n_hid = mesh.shape["tok"], mesh.shape["hid"]
    grouped = n_tok == 16 and n_hid == 2
    if grouped:
        tok = ("ah", "bh", "bl", "al")
        inner = Mesh(mesh.devices.reshape(2, 2, 2, 2, n_hid), tok + ("hid",))
    else:
        tok, inner = "tok", mesh

    def local(tokens, ffn_gain, w_in, w_out, conv_gain, *rest):
        if grouped:
            *rest, lengths = rest
            utter = utterances(tokens.shape[0], tok, lengths)
            mid_own, mid_full, utter = grouped_ffn(tokens, ffn_gain, w_in, w_out, utter)
            return grouped_conv_module(mid_own, mid_full, tok, utter, conv_gain, *rest)
        mid_own, mid_full = gathered_ffn(tokens, ffn_gain, w_in, w_out)
        return conv_module(mid_own, mid_full, tok, conv_gain, *rest)

    placed = (
        P(tok, "hid"),
        P(),
        P(tok, "hid"),
        P("hid", tok),
        P(),
        P(None, "hid"),
        P(None, "hid"),
        P(None, "hid"),
        P("hid"),
        P("hid"),
        P(None, "hid"),
        P(),
    )
    return jax.shard_map(
        local, mesh=inner, in_specs=placed, out_specs=P(tok, "hid"), check_vma=False
    )
```

```python
import functools

import jax
import jax.numpy as jnp
from jax import lax
from jax.experimental import pallas as pl
from jax.experimental.pallas import tpu as pltpu
from jax.sharding import Mesh, PartitionSpec as P

SWAP = [(0, 1), (1, 0)]


def norm_rows(values, gain):
    mean = jnp.mean(values, axis=-1, keepdims=True)
    centred = values - mean
    var = jnp.mean(centred * centred, axis=-1, keepdims=True)
    return centred * lax.rsqrt(var + 1e-05) * gain


def padded(cells, axis, width):
    count = lax.axis_size(axis)
    ends = count - 1
    head = cells[:width]
    tail = cells[cells.shape[0] - width :]
    return jnp.concatenate(
        [
            lax.ppermute(tail, axis, [(i, (i + 1) % count) for i in range(ends)]),
            cells,
            lax.ppermute(head, axis, [((i + 1) % count, i) for i in range(ends)]),
        ],
        axis=0,
    )


def conv_module(mid_own, mid_full, axis, conv_gain, w_value, w_gate, depth_kernel, bn_scale, bn_shift, w_proj, lengths):
    rows, width = mid_own.shape
    mid_normed = norm_rows(mid_full.astype(jnp.float32), conv_gain).astype(jnp.bfloat16)
    value = jnp.dot(mid_normed, w_value, preferred_element_type=jnp.float32)
    gate = jnp.dot(mid_normed, w_gate, preferred_element_type=jnp.float32)
    glu = (value * jax.nn.sigmoid(gate)).astype(jnp.bfloat16)
    extended = padded(glu, axis, 16).astype(jnp.float32)
    ends = jnp.cumsum(lengths)
    first_row = lax.axis_index(axis) * rows - 16
    positions = first_row + jnp.arange(rows + 32, dtype=jnp.int32)
    utter = jnp.sum((ends[None, :] <= positions[:, None]).astype(jnp.int32), axis=1)
    centre = utter[16 : 16 + rows]
    conv = jnp.zeros((rows, width), jnp.float32)
    for tap in range(depth_kernel.shape[0]):
        same = (utter[tap + 1 : tap + 1 + rows] == centre)[:, None]
        conv = conv + jnp.where(
            same, extended[tap + 1 : tap + 1 + rows] * depth_kernel[tap][None, :], 0.0
        )
    act = jax.nn.silu(conv * bn_scale + bn_shift).astype(jnp.bfloat16)
    act_full = lax.all_gather(act, "hid", axis=1, tiled=True)
    projected = jnp.dot(act_full, w_proj, preferred_element_type=jnp.float32)
    return (mid_own.astype(jnp.float32) + projected).astype(jnp.bfloat16)


def gathered_ffn(tokens, ffn_gain, w_in, w_out):
    whole = lax.all_gather(tokens, "hid", axis=1, tiled=True)
    normed = norm_rows(whole.astype(jnp.float32), ffn_gain).astype(jnp.bfloat16)
    pre = jnp.dot(
        normed, lax.all_gather(w_in, "tok", axis=0, tiled=True), preferred_element_type=jnp.float32
    )
    hidden = jax.nn.silu(pre).astype(jnp.bfloat16)
    partial_sum = jnp.dot(
        hidden, lax.all_gather(w_out, "tok", axis=1, tiled=True), preferred_element_type=jnp.float32
    )
    share = lax.psum_scatter(
        partial_sum.astype(jnp.bfloat16), "hid", scatter_dimension=1, tiled=True
    ).astype(jnp.float32)
    mid_own = (tokens.astype(jnp.float32) + 0.5 * share).astype(jnp.bfloat16)
    return mid_own, lax.all_gather(mid_own, "hid", axis=1, tiled=True)


GROUP = ("bh", "bl")
VMEM_LIMIT = 40 * 2**20
VMEM = pl.BlockSpec(memory_space=pltpu.VMEM)
SMEM = pl.BlockSpec(memory_space=pltpu.SMEM)


def kernel_call(body, outs, ins, scratch=(), scalars=0, flops=0, moved=0):
    return pl.pallas_call(
        body,
        out_shape=[jax.ShapeDtypeStruct(shape, dtype) for shape, dtype in outs],
        in_specs=[SMEM] * scalars + [VMEM] * (len(ins) - scalars),
        out_specs=[VMEM] * len(outs),
        scratch_shapes=list(scratch),
        compiler_params=pltpu.CompilerParams(vmem_limit_bytes=VMEM_LIMIT),
        cost_estimate=pl.CostEstimate(flops=flops, bytes_accessed=moved, transcendentals=0),
    )(*ins)


def f32(values):
    return values.astype(jnp.float32)


def silu(values):
    return values / (1.0 + jnp.exp(-values))


def cut_kernel(*refs):
    *arrays, out_ref = refs
    parts, _, width = out_ref.shape
    for part in range(parts):
        at = 0
        for ref in arrays:
            rows = ref.shape[0]
            out_ref[part, at : at + rows, :] = ref[:, part * width : (part + 1) * width]
            at += rows


def part_kernel(both_ref, first_ref, second_ref):
    half = first_ref.shape[0]
    first_ref[...] = both_ref[:half]
    second_ref[...] = both_ref[half:]


def norm_kernel(start_ref, whole_ref, gain_ref, mine_ref, out_ref):
    rows = mine_ref.shape[0]
    mine = whole_ref[pl.ds(pl.multiple_of(start_ref[0], rows), rows), :]
    mine_ref[...] = mine
    out_ref[...] = norm_rows(f32(mine), gain_ref[...]).astype(jnp.bfloat16)


def join_kernel(*refs):
    *pieces, out_ref = refs
    rows = pieces[0].shape[0]
    for i, piece in enumerate(pieces):
        out_ref[i * rows : (i + 1) * rows] = piece[...]


def interleave(full_ref, base, block, own_refs, other_refs, me_l, skip=0):
    for refs, turn in ((own_refs, me_l), (other_refs, 1 - me_l)):
        blocks = [(ref, j) for ref in refs for j in range(ref.shape[0])]
        for i, (ref, j) in enumerate(blocks):
            at = pl.multiple_of(base + (2 * i + turn) * block, block)
            full_ref[pl.ds(at, block), :] = ref[j, skip : skip + block, :]


def hidden_kernel(me_ref, x_ref, b_ref, bx_ref, h_ref, w_ref):
    me_l, me_a = me_ref[0], me_ref[2]
    part, block = w_ref.shape[0] // 2, b_ref.shape[1] // 2
    interleave(w_ref, me_a * part, block, [b_ref], [bx_ref], me_l)
    interleave(w_ref, (1 - me_a) * part, block, [b_ref], [bx_ref], me_l, block)
    step = 256
    for at in range(0, x_ref.shape[0], step):
        pre = jnp.dot(x_ref[at : at + step, :], w_ref[...], preferred_element_type=jnp.float32)
        h_ref[at : at + step, :] = silu(pre).astype(jnp.bfloat16)


def sums_kernel(n_own, me_ref, own_ref, oth_ref, *refs):
    *blocks, kept_ref, sent_ref, w_ref = refs
    interleave(w_ref, 0, blocks[0].shape[1], blocks[:n_own], blocks[n_own:], me_ref[0])
    step = 256
    for h_ref, out_ref in ((oth_ref, sent_ref), (own_ref, kept_ref)):
        for at in range(0, h_ref.shape[0], step):
            out_ref[at : at + step, :] = lax.dot_general(
                h_ref[at : at + step, :],
                w_ref[...],
                (((1,), (1,)), ((), ())),
                preferred_element_type=jnp.float32,
            ).astype(out_ref.dtype)


def add_kernel(kept_ref, came_ref, *out_refs):
    rows = out_refs[0].shape[0]
    for k, out_ref in enumerate(out_refs):
        at = slice(k * rows, (k + 1) * rows)
        out_ref[...] = (kept_ref[at, :] + f32(came_ref[at, :])).astype(out_ref.dtype)


def mid_kernel(me_ref, mine_ref, *refs):
    *sums, out_ref = refs
    for place, part in ((me_ref[2], sums[:4]), (1 - me_ref[2], sums[4:])):
        total = part[0][...]
        for other in part[1:]:
            total = total + f32(other[...])
        width = part[0].shape[1]
        at = pl.ds(pl.multiple_of(place * width, width), width)
        out_ref[:, at] = (f32(mine_ref[:, at]) + 0.5 * total).astype(jnp.bfloat16)


HALO = 16


def utter_kernel(first_ref, lengths_ref, out_ref, base_ref):
    position = first_ref[0] + lax.broadcasted_iota(jnp.int32, base_ref.shape, 0)

    def step(u, carry):
        end, utter = carry
        end = end + lengths_ref[u]
        return end, utter + jnp.where(position >= end, 1, 0)

    zero = jnp.zeros(base_ref.shape, jnp.int32)
    base_ref[...] = lax.fori_loop(0, lengths_ref.shape[0], step, (jnp.int32(0), zero))[1]
    for r in range(8):
        out_ref[r] = base_ref[1 + r : 1 + r + out_ref.shape[1], :]


def glu_kernel(mid_ref, gain_ref, value_ref, gate_ref, glu_ref, head_ref, tail_ref):
    normed = norm_rows(f32(mid_ref[...]), gain_ref[...]).astype(jnp.bfloat16)
    value = jnp.dot(normed, value_ref[...], preferred_element_type=jnp.float32)
    gate = jnp.dot(normed, gate_ref[...], preferred_element_type=jnp.float32)
    glu = (value / (1.0 + jnp.exp(-gate))).astype(jnp.bfloat16)
    glu_ref[...] = glu
    head_ref[...] = glu[:HALO]
    tail_ref[...] = glu[glu.shape[0] - HALO :]


def conv_rows(ext_ref, utter_ref, taps_ref, scale_ref, shift_ref, out_ref, tiles, step):
    width = out_ref.shape[1]
    taps = taps_ref.shape[0]
    lanes = 128
    group = 3 if width % (3 * lanes) == 0 else 1
    span = step + taps - 8

    def columns(i, _):
        at_lane = [pl.ds(pl.multiple_of((i * group + g) * lanes, lanes), lanes) for g in range(group)]
        for ext_at, at, out_at in tiles:
            centre = utter_ref[7, at + HALO - 8 : at + HALO - 8 + step, :]
            totals = [jnp.zeros((step, lanes), jnp.float32)] * group
            for r in range(8):
                cells = [ext_ref[ext_at + 1 + r : ext_at + 1 + r + span, c] for c in at_lane]
                for q in range(0, taps, 8):
                    same = utter_ref[r, at + q : at + q + step, :] == centre
                    for g, c in enumerate(at_lane):
                        term = cells[g][q : q + step] * taps_ref[q + r : q + r + 1, c]
                        totals[g] = totals[g] + jnp.where(same, term, 0.0)
            for total, c in zip(totals, at_lane):
                act = silu(total * scale_ref[:, c] + shift_ref[:, c])
                out_ref[out_at : out_at + step, c] = act.astype(out_ref.dtype)
        return 0

    lax.fori_loop(0, width // (group * lanes), columns, 0)


def inner_conv_kernel(glu_ref, utter_ref, taps_ref, scale_ref, shift_ref, out_ref, ext_ref):
    ext_ref[...] = f32(glu_ref[...])
    step = 2 * HALO
    tiles = [(at - HALO, at, at) for at in range(HALO, out_ref.shape[0] - HALO, step)]
    conv_rows(ext_ref, utter_ref, taps_ref, scale_ref, shift_ref, out_ref, tiles, step)


def edge_conv_kernel(
    act_ref, top_ref, glu_ref, bottom_ref, utter_ref, taps_ref, scale_ref, shift_ref, out_ref, ext_ref
):
    rows = out_ref.shape[0]
    last = rows - HALO
    out_ref[HALO:last, :] = act_ref[HALO:last, :]
    ext_ref[:HALO, :] = f32(top_ref[...])
    ext_ref[HALO : 3 * HALO, :] = f32(glu_ref[: 2 * HALO, :])
    ext_ref[3 * HALO : 5 * HALO, :] = f32(glu_ref[rows - 2 * HALO :, :])
    ext_ref[5 * HALO :, :] = f32(bottom_ref[...])
    tiles = [(0, 0, 0), (3 * HALO, last, last)]
    conv_rows(ext_ref, utter_ref, taps_ref, scale_ref, shift_ref, out_ref, tiles, HALO)


def utterances(rows, axis, lengths, taps):
    return kernel_call(
        utter_kernel,
        [((8, rows + taps - 8, 128), jnp.int32)],
        [(lax.axis_index(axis) * rows - HALO)[None], lengths],
        scratch=[pltpu.VMEM((rows + 2 * HALO, 128), jnp.int32)],
        scalars=2,
    )[0]


def grouped_conv_module(mid_own, mid_full, axis, early, w_value, w_gate, depth_kernel, w_proj):
    rows, width = mid_own.shape
    utter, conv_gain, bn_scale, bn_shift = early
    bf16 = jnp.bfloat16
    glu, head, tail = kernel_call(
        glu_kernel,
        [((rows, width), bf16)] + [((HALO, width), bf16)] * 2,
        [mid_full, conv_gain, w_value, w_gate],
        flops=4 * rows * w_value.size,
        moved=4 * w_value.size,
    )
    count = lax.axis_size(axis)
    top = lax.ppermute(tail, axis, [(i, i + 1) for i in range(count - 1)])
    bottom = lax.ppermute(head, axis, [(i + 1, i) for i in range(count - 1)])
    rest = [utter, depth_kernel, bn_scale, bn_shift]
    (act,) = kernel_call(
        inner_conv_kernel,
        [((rows, width), bf16)],
        [glu, *rest],
        scratch=[pltpu.VMEM((rows, width), jnp.float32)],
        flops=rows * depth_kernel.size,
        moved=16 * rows * width,
    )
    (act,) = kernel_call(
        edge_conv_kernel,
        [((rows, width), bf16)],
        [act, top, glu, bottom, *rest],
        scratch=[pltpu.VMEM((6 * HALO, width), jnp.float32)],
        flops=HALO * depth_kernel.size,
        moved=4 * rows * width,
    )
    act_full = lax.all_gather(act, "hid", axis=1, tiled=True)
    projected = jnp.dot(act_full, w_proj, preferred_element_type=jnp.float32)
    return (mid_own.astype(jnp.float32) + projected).astype(jnp.bfloat16)


def partner(values, step):
    return lax.ppermute(values, GROUP, [(i, i ^ step) for i in range(4)])


def swap(values, axis):
    return lax.ppermute(values, axis, SWAP)


def recut(parts):
    return lax.all_to_all(parts, GROUP, 0, 0)


def grouped_ffn(tokens, ffn_gain, w_in, w_out, early):
    rows, width = tokens.shape
    half = rows // 2
    shard, hid = w_in.shape
    wide = 2 * width
    units = hid // 4
    bf16 = jnp.bfloat16
    me_c = lax.axis_index("hid")
    me = jnp.stack([lax.axis_index("al"), me_c, lax.axis_index("ah")])
    tie = lax.optimization_barrier

    block, pair = (4, shard, units), (2, shard, units)
    in_far = swap(w_in, "ah")
    (out_cut,) = kernel_call(cut_kernel, [(block, bf16)], [w_out.T])
    out_o = recut(out_cut)
    whole = lax.all_gather(tokens, "hid", axis=1, tiled=True)
    mine, normed = kernel_call(
        norm_kernel,
        [((half, wide), bf16)] * 2,
        [(me_c * half)[None], whole, ffn_gain[None, :]],
        scalars=1,
    )
    frames1 = partner(normed, 1)
    in_far, out_o, normed, frames1, early = tie((in_far, out_o, normed, frames1, early))
    (in_both,) = kernel_call(cut_kernel, [((4, 2 * shard, units), bf16)], [w_in, in_far])
    in_b = recut(in_both)
    out_1, out_2 = kernel_call(part_kernel, [(pair, bf16)] * 2, [out_o])
    out_z1 = swap(out_1, "ah")
    out_x = swap(out_o, "al")
    in_b, out_z1, out_2, out_o, out_x, normed = tie((in_b, out_z1, out_2, out_o, out_x, normed))
    in_bx = swap(in_b, "al")
    out_z2 = swap(out_2, "ah")
    frames2 = partner(normed, 2)
    frames3 = partner(normed, 3)
    out_z1, out_z2, in_bx, frames2, frames3 = tie((out_z1, out_z2, in_bx, frames2, frames3))
    out_zx1 = swap(out_z1, "al")
    out_zx2 = swap(out_z2, "al")
    (x_own,) = kernel_call(
        join_kernel, [((4 * half, wide), bf16)], [normed, frames1, frames2, frames3]
    )
    x_oth = swap(x_own, "hid")

    def units_of(x):
        return kernel_call(
            hidden_kernel,
            [((4 * half, units), bf16)],
            [me, x, in_b, in_bx],
            scratch=[pltpu.VMEM((wide, units), bf16)],
            scalars=1,
        )[0]

    hidden = [units_of(x_own), units_of(x_oth)]

    def products(own, other):
        return kernel_call(
            functools.partial(sums_kernel, len(own)),
            [((4 * half, width), jnp.float32), ((4 * half, width), bf16)],
            [me, *hidden, *own, *other],
            scratch=[pltpu.VMEM((width, units), bf16)],
            scalars=1,
        )

    def scatter(kept, sent):
        total = kernel_call(
            add_kernel,
            [((half, width), jnp.float32)] + [((half, width), bf16)] * 3,
            [kept, swap(sent, "hid")],
        )
        return [total[0]] + [partner(v, k + 1) for k, v in enumerate(total[1:])]

    near, out_zx1, out_zx2 = tie((products([out_o], [out_x]), out_zx1, out_zx2))
    far = products([out_z1, out_z2], [out_zx1, out_zx2])
    (mid_rows,) = kernel_call(
        mid_kernel, [((half, wide), bf16)], [me, mine, *scatter(*near), *scatter(*far)], scalars=1
    )
    mid_full = lax.all_gather(mid_rows, "hid", axis=0, tiled=True)
    mid_own = lax.dynamic_slice_in_dim(mid_full, me_c * width, width, 1)
    return mid_own, mid_full, early


def solution(mesh):
    n_tok, n_hid = mesh.shape["tok"], mesh.shape["hid"]
    grouped = n_tok == 16 and n_hid == 2
    if grouped:
        tok = ("ah", "bh", "bl", "al")
        inner = Mesh(mesh.devices.reshape(2, 2, 2, 2, n_hid), tok + ("hid",))
    else:
        tok, inner = "tok", mesh

    def local(tokens, ffn_gain, w_in, w_out, conv_gain, *rest):
        if grouped:
            w_value, w_gate, depth_kernel, bn_scale, bn_shift, w_proj, lengths = rest
            utter = utterances(tokens.shape[0], tok, lengths, depth_kernel.shape[0])
            early = utter, conv_gain[None, :], bn_scale[None, :], bn_shift[None, :]
            mid_own, mid_full, early = grouped_ffn(tokens, ffn_gain, w_in, w_out, early)
            return grouped_conv_module(
                mid_own, mid_full, tok, early, w_value, w_gate, depth_kernel, w_proj
            )
        mid_own, mid_full = gathered_ffn(tokens, ffn_gain, w_in, w_out)
        return conv_module(mid_own, mid_full, tok, conv_gain, *rest)

    placed = (
        P(tok, "hid"),
        P(),
        P(tok, "hid"),
        P("hid", tok),
        P(),
        P(None, "hid"),
        P(None, "hid"),
        P(None, "hid"),
        P("hid"),
        P("hid"),
        P(None, "hid"),
        P(),
    )
    return jax.shard_map(
        local, mesh=inner, in_specs=placed, out_specs=P(tok, "hid"), check_vma=False
    )
```

```python
import functools

import jax
import jax.numpy as jnp
from jax import lax
from jax.experimental import pallas as pl
from jax.experimental.pallas import tpu as pltpu
from jax.sharding import Mesh, PartitionSpec as P

SWAP = [(0, 1), (1, 0)]


def norm_rows(values, gain):
    mean = jnp.mean(values, axis=-1, keepdims=True)
    centred = values - mean
    var = jnp.mean(centred * centred, axis=-1, keepdims=True)
    return centred * lax.rsqrt(var + 1e-05) * gain


def padded(cells, axis, width):
    count = lax.axis_size(axis)
    ends = count - 1
    head = cells[:width]
    tail = cells[cells.shape[0] - width :]
    return jnp.concatenate(
        [
            lax.ppermute(tail, axis, [(i, (i + 1) % count) for i in range(ends)]),
            cells,
            lax.ppermute(head, axis, [((i + 1) % count, i) for i in range(ends)]),
        ],
        axis=0,
    )


def conv_module(mid_own, mid_full, axis, conv_gain, w_value, w_gate, depth_kernel, bn_scale, bn_shift, w_proj, lengths):
    rows, width = mid_own.shape
    mid_normed = norm_rows(mid_full.astype(jnp.float32), conv_gain).astype(jnp.bfloat16)
    value = jnp.dot(mid_normed, w_value, preferred_element_type=jnp.float32)
    gate = jnp.dot(mid_normed, w_gate, preferred_element_type=jnp.float32)
    glu = (value * jax.nn.sigmoid(gate)).astype(jnp.bfloat16)
    extended = padded(glu, axis, 16).astype(jnp.float32)
    ends = jnp.cumsum(lengths)
    first_row = lax.axis_index(axis) * rows - 16
    positions = first_row + jnp.arange(rows + 32, dtype=jnp.int32)
    utter = jnp.sum((ends[None, :] <= positions[:, None]).astype(jnp.int32), axis=1)
    centre = utter[16 : 16 + rows]
    conv = jnp.zeros((rows, width), jnp.float32)
    for tap in range(depth_kernel.shape[0]):
        same = (utter[tap + 1 : tap + 1 + rows] == centre)[:, None]
        conv = conv + jnp.where(
            same, extended[tap + 1 : tap + 1 + rows] * depth_kernel[tap][None, :], 0.0
        )
    act = jax.nn.silu(conv * bn_scale + bn_shift).astype(jnp.bfloat16)
    act_full = lax.all_gather(act, "hid", axis=1, tiled=True)
    projected = jnp.dot(act_full, w_proj, preferred_element_type=jnp.float32)
    return (mid_own.astype(jnp.float32) + projected).astype(jnp.bfloat16)


def gathered_ffn(tokens, ffn_gain, w_in, w_out):
    whole = lax.all_gather(tokens, "hid", axis=1, tiled=True)
    normed = norm_rows(whole.astype(jnp.float32), ffn_gain).astype(jnp.bfloat16)
    pre = jnp.dot(
        normed, lax.all_gather(w_in, "tok", axis=0, tiled=True), preferred_element_type=jnp.float32
    )
    hidden = jax.nn.silu(pre).astype(jnp.bfloat16)
    partial_sum = jnp.dot(
        hidden, lax.all_gather(w_out, "tok", axis=1, tiled=True), preferred_element_type=jnp.float32
    )
    share = lax.psum_scatter(
        partial_sum.astype(jnp.bfloat16), "hid", scatter_dimension=1, tiled=True
    ).astype(jnp.float32)
    mid_own = (tokens.astype(jnp.float32) + 0.5 * share).astype(jnp.bfloat16)
    return mid_own, lax.all_gather(mid_own, "hid", axis=1, tiled=True)


GROUP = ("bh", "bl")
VMEM_LIMIT = 40 * 2**20
VMEM = pl.BlockSpec(memory_space=pltpu.VMEM)
SMEM = pl.BlockSpec(memory_space=pltpu.SMEM)


def kernel_call(body, outs, ins, scratch=(), scalars=0, flops=0, moved=0):
    return pl.pallas_call(
        body,
        out_shape=[jax.ShapeDtypeStruct(shape, dtype) for shape, dtype in outs],
        in_specs=[SMEM] * scalars + [VMEM] * (len(ins) - scalars),
        out_specs=[VMEM] * len(outs),
        scratch_shapes=list(scratch),
        compiler_params=pltpu.CompilerParams(vmem_limit_bytes=VMEM_LIMIT),
        cost_estimate=pl.CostEstimate(flops=flops, bytes_accessed=moved, transcendentals=0),
    )(*ins)


def f32(values):
    return values.astype(jnp.float32)


def silu(values):
    return values / (1.0 + jnp.exp(-values))


def cut_kernel(*refs):
    *arrays, out_ref = refs
    parts, _, width = out_ref.shape
    for part in range(parts):
        at = 0
        for ref in arrays:
            rows = ref.shape[0]
            out_ref[part, at : at + rows, :] = ref[:, part * width : (part + 1) * width]
            at += rows


def part_kernel(both_ref, first_ref, second_ref):
    half, shard, _ = first_ref.shape
    skip = both_ref.shape[1] - shard
    first_ref[...] = both_ref[:half, skip:, :]
    second_ref[...] = both_ref[half:, skip:, :]


def norm_kernel(start_ref, whole_ref, gain_ref, mine_ref, out_ref):
    rows = mine_ref.shape[0]
    mine = whole_ref[pl.ds(pl.multiple_of(start_ref[0], rows), rows), :]
    mine_ref[...] = mine
    out_ref[...] = norm_rows(f32(mine), gain_ref[...]).astype(jnp.bfloat16)


def join_kernel(*refs):
    *pieces, out_ref = refs
    rows = pieces[0].shape[0]
    for i, piece in enumerate(pieces):
        out_ref[i * rows : (i + 1) * rows] = piece[...]


def interleave(full_ref, base, block, own_refs, other_refs, me_l, last=False):
    for refs, turn in ((own_refs, me_l), (other_refs, 1 - me_l)):
        blocks = [(ref, j) for ref in refs for j in range(ref.shape[0])]
        for i, (ref, j) in enumerate(blocks):
            at = pl.multiple_of(base + (2 * i + turn) * block, block)
            skip = ref.shape[1] - block if last else 0
            full_ref[pl.ds(at, block), :] = ref[j, skip : skip + block, :]


def hidden_kernel(me_ref, x_ref, both_ref, both_x_ref, z_ref, zx_ref, h_ref, w_ref):
    me_l, me_a = me_ref[0], me_ref[2]
    part, block = w_ref.shape[0] // 2, z_ref.shape[1]
    interleave(w_ref, me_a * part, block, [both_ref], [both_x_ref], me_l)
    interleave(w_ref, (1 - me_a) * part, block, [z_ref], [zx_ref], me_l)
    step = 256
    for at in range(0, x_ref.shape[0], step):
        pre = jnp.dot(x_ref[at : at + step, :], w_ref[...], preferred_element_type=jnp.float32)
        h_ref[at : at + step, :] = silu(pre).astype(jnp.bfloat16)


def sums_kernel(n_own, me_ref, own_ref, oth_ref, *refs):
    *blocks, kept_ref, sent_ref, w_ref = refs
    block = w_ref.shape[0] // 8
    interleave(w_ref, 0, block, blocks[:n_own], blocks[n_own:], me_ref[0], True)
    step = 256
    for h_ref, out_ref in ((oth_ref, sent_ref), (own_ref, kept_ref)):
        for at in range(0, h_ref.shape[0], step):
            out_ref[at : at + step, :] = lax.dot_general(
                h_ref[at : at + step, :],
                w_ref[...],
                (((1,), (1,)), ((), ())),
                preferred_element_type=jnp.float32,
            ).astype(out_ref.dtype)


def add_kernel(kept_ref, came_ref, *out_refs):
    rows = out_refs[0].shape[0]
    for k, out_ref in enumerate(out_refs):
        at = slice(k * rows, (k + 1) * rows)
        out_ref[...] = (kept_ref[at, :] + f32(came_ref[at, :])).astype(out_ref.dtype)


def mid_kernel(me_ref, mine_ref, *refs):
    *sums, out_ref = refs
    for place, part in ((me_ref[2], sums[:4]), (1 - me_ref[2], sums[4:])):
        total = part[0][...]
        for other in part[1:]:
            total = total + f32(other[...])
        width = part[0].shape[1]
        at = pl.ds(pl.multiple_of(place * width, width), width)
        out_ref[:, at] = (f32(mine_ref[:, at]) + 0.5 * total).astype(jnp.bfloat16)


HALO = 16


def utter_kernel(first_ref, lengths_ref, out_ref, base_ref):
    position = first_ref[0] + lax.broadcasted_iota(jnp.int32, base_ref.shape, 0)

    def step(u, carry):
        end, utter = carry
        end = end + lengths_ref[u]
        return end, utter + jnp.where(position >= end, 1, 0)

    zero = jnp.zeros(base_ref.shape, jnp.int32)
    base_ref[...] = lax.fori_loop(0, lengths_ref.shape[0], step, (jnp.int32(0), zero))[1]
    for r in range(8):
        out_ref[r] = base_ref[1 + r : 1 + r + out_ref.shape[1], :]


def glu_kernel(mid_ref, gain_ref, value_ref, gate_ref, glu_ref, head_ref, tail_ref):
    normed = norm_rows(f32(mid_ref[...]), gain_ref[...]).astype(jnp.bfloat16)
    value = jnp.dot(normed, value_ref[...], preferred_element_type=jnp.float32)
    gate = jnp.dot(normed, gate_ref[...], preferred_element_type=jnp.float32)
    glu = (value / (1.0 + jnp.exp(-gate))).astype(jnp.bfloat16)
    glu_ref[...] = glu
    head_ref[...] = glu[:HALO]
    tail_ref[...] = glu[glu.shape[0] - HALO :]


def conv_rows(ext_ref, utter_ref, taps_ref, scale_ref, shift_ref, out_ref, tiles, step):
    width = out_ref.shape[1]
    taps = taps_ref.shape[0]
    lanes = 128
    group = 3 if width % (3 * lanes) == 0 else 1
    span = step + taps - 8

    def columns(i, _):
        at_lane = [pl.ds(pl.multiple_of((i * group + g) * lanes, lanes), lanes) for g in range(group)]
        for ext_at, at, out_at in tiles:
            centre = utter_ref[7, at + HALO - 8 : at + HALO - 8 + step, :]
            totals = [jnp.zeros((step, lanes), jnp.float32)] * group
            for r in range(8):
                cells = [ext_ref[ext_at + 1 + r : ext_at + 1 + r + span, c] for c in at_lane]
                for q in range(0, taps, 8):
                    same = utter_ref[r, at + q : at + q + step, :] == centre
                    for g, c in enumerate(at_lane):
                        term = cells[g][q : q + step] * taps_ref[q + r : q + r + 1, c]
                        totals[g] = totals[g] + jnp.where(same, term, 0.0)
            for total, c in zip(totals, at_lane):
                act = silu(total * scale_ref[:, c] + shift_ref[:, c])
                out_ref[out_at : out_at + step, c] = act.astype(out_ref.dtype)
        return 0

    lax.fori_loop(0, width // (group * lanes), columns, 0)


def inner_conv_kernel(glu_ref, utter_ref, taps_ref, scale_ref, shift_ref, out_ref, ext_ref):
    ext_ref[...] = f32(glu_ref[...])
    step = 2 * HALO
    tiles = [(at - HALO, at, at) for at in range(HALO, out_ref.shape[0] - HALO, step)]
    conv_rows(ext_ref, utter_ref, taps_ref, scale_ref, shift_ref, out_ref, tiles, step)


def edge_conv_kernel(
    act_ref, top_ref, glu_ref, bottom_ref, utter_ref, taps_ref, scale_ref, shift_ref, out_ref, ext_ref
):
    rows = out_ref.shape[0]
    last = rows - HALO
    out_ref[HALO:last, :] = act_ref[HALO:last, :]
    ext_ref[:HALO, :] = f32(top_ref[...])
    ext_ref[HALO : 3 * HALO, :] = f32(glu_ref[: 2 * HALO, :])
    ext_ref[3 * HALO : 5 * HALO, :] = f32(glu_ref[rows - 2 * HALO :, :])
    ext_ref[5 * HALO :, :] = f32(bottom_ref[...])
    tiles = [(0, 0, 0), (3 * HALO, last, last)]
    conv_rows(ext_ref, utter_ref, taps_ref, scale_ref, shift_ref, out_ref, tiles, HALO)


def utterances(rows, axis, lengths, taps):
    return kernel_call(
        utter_kernel,
        [((8, rows + taps - 8, 128), jnp.int32)],
        [(lax.axis_index(axis) * rows - HALO)[None], lengths],
        scratch=[pltpu.VMEM((rows + 2 * HALO, 128), jnp.int32)],
        scalars=2,
    )[0]


def grouped_conv_module(mid_own, mid_full, axis, early, w_value, w_gate, depth_kernel, w_proj):
    rows, width = mid_own.shape
    utter, conv_gain, bn_scale, bn_shift = early
    bf16 = jnp.bfloat16
    glu, head, tail = kernel_call(
        glu_kernel,
        [((rows, width), bf16)] + [((HALO, width), bf16)] * 2,
        [mid_full, conv_gain, w_value, w_gate],
        flops=4 * rows * w_value.size,
        moved=4 * w_value.size,
    )
    count = lax.axis_size(axis)
    top = lax.ppermute(tail, axis, [(i, i + 1) for i in range(count - 1)])
    bottom = lax.ppermute(head, axis, [(i + 1, i) for i in range(count - 1)])
    rest = [utter, depth_kernel, bn_scale, bn_shift]
    (act,) = kernel_call(
        inner_conv_kernel,
        [((rows, width), bf16)],
        [glu, *rest],
        scratch=[pltpu.VMEM((rows, width), jnp.float32)],
        flops=rows * depth_kernel.size,
        moved=16 * rows * width,
    )
    (act,) = kernel_call(
        edge_conv_kernel,
        [((rows, width), bf16)],
        [act, top, glu, bottom, *rest],
        scratch=[pltpu.VMEM((6 * HALO, width), jnp.float32)],
        flops=HALO * depth_kernel.size,
        moved=4 * rows * width,
    )
    act_full = lax.all_gather(act, "hid", axis=1, tiled=True)
    projected = jnp.dot(act_full, w_proj, preferred_element_type=jnp.float32)
    return (mid_own.astype(jnp.float32) + projected).astype(jnp.bfloat16)


def partner(values, step):
    return lax.ppermute(values, GROUP, [(i, i ^ step) for i in range(4)])


def swap(values, axis):
    return lax.ppermute(values, axis, SWAP)


def recut(parts):
    return lax.all_to_all(parts, GROUP, 0, 0)


def grouped_ffn(tokens, ffn_gain, w_in, w_out, early):
    rows, width = tokens.shape
    half = rows // 2
    shard, hid = w_in.shape
    wide = 2 * width
    units = hid // 4
    bf16 = jnp.bfloat16
    me_c = lax.axis_index("hid")
    me = jnp.stack([lax.axis_index("al"), me_c, lax.axis_index("ah")])
    tie = lax.optimization_barrier

    block, pair = (4, shard, units), (2, shard, units)
    in_far = swap(w_in, "ah")
    (both,) = kernel_call(cut_kernel, [((4, 2 * shard, units), bf16)], [w_in, w_out.T])
    both = recut(both)
    whole = lax.all_gather(tokens, "hid", axis=1, tiled=True)
    mine, normed = kernel_call(
        norm_kernel,
        [((half, wide), bf16)] * 2,
        [(me_c * half)[None], whole, ffn_gain[None, :]],
        scalars=1,
    )
    frames1 = partner(normed, 1)
    in_far, both, normed, frames1, early = tie((in_far, both, normed, frames1, early))
    both_x = swap(both, "al")
    (in_z,) = kernel_call(cut_kernel, [(block, bf16)], [in_far])
    in_z = recut(in_z)
    out_1, out_2 = kernel_call(part_kernel, [(pair, bf16)] * 2, [both])
    out_z1 = swap(out_1, "ah")
    frames3 = partner(normed, 3)
    both_x, in_z = tie((both_x, in_z))
    out_z1, out_2, normed, frames3 = tie((out_z1, out_2, normed, frames3))
    in_zx = swap(in_z, "al")
    out_z2 = swap(out_2, "ah")
    frames2 = partner(normed, 2)
    in_zx, out_z1, out_z2, frames2 = tie((in_zx, out_z1, out_z2, frames2))
    out_zx1 = swap(out_z1, "al")
    out_zx2 = swap(out_z2, "al")
    (x_own,) = kernel_call(
        join_kernel, [((4 * half, wide), bf16)], [normed, frames1, frames2, frames3]
    )
    x_oth = swap(x_own, "hid")

    def units_of(x):
        return kernel_call(
            hidden_kernel,
            [((4 * half, units), bf16)],
            [me, x, both, both_x, in_z, in_zx],
            scratch=[pltpu.VMEM((wide, units), bf16)],
            scalars=1,
        )[0]

    hidden = [units_of(x_own), units_of(x_oth)]

    def products(own, other):
        return kernel_call(
            functools.partial(sums_kernel, len(own)),
            [((4 * half, width), jnp.float32), ((4 * half, width), bf16)],
            [me, *hidden, *own, *other],
            scratch=[pltpu.VMEM((width, units), bf16)],
            scalars=1,
        )

    def scatter(kept, sent):
        total = kernel_call(
            add_kernel,
            [((half, width), jnp.float32)] + [((half, width), bf16)] * 3,
            [kept, swap(sent, "hid")],
        )
        return [total[0]] + [partner(v, k + 1) for k, v in enumerate(total[1:])]

    near, out_zx1, out_zx2 = tie((products([both], [both_x]), out_zx1, out_zx2))
    far = products([out_z1, out_z2], [out_zx1, out_zx2])
    (mid_rows,) = kernel_call(
        mid_kernel, [((half, wide), bf16)], [me, mine, *scatter(*near), *scatter(*far)], scalars=1
    )
    mid_full = lax.all_gather(mid_rows, "hid", axis=0, tiled=True)
    mid_own = lax.dynamic_slice_in_dim(mid_full, me_c * width, width, 1)
    return mid_own, mid_full, early


def solution(mesh):
    n_tok, n_hid = mesh.shape["tok"], mesh.shape["hid"]
    grouped = n_tok == 16 and n_hid == 2
    if grouped:
        tok = ("ah", "bh", "bl", "al")
        inner = Mesh(mesh.devices.reshape(2, 2, 2, 2, n_hid), tok + ("hid",))
    else:
        tok, inner = "tok", mesh

    def local(tokens, ffn_gain, w_in, w_out, conv_gain, *rest):
        if grouped:
            w_value, w_gate, depth_kernel, bn_scale, bn_shift, w_proj, lengths = rest
            utter = utterances(tokens.shape[0], tok, lengths, depth_kernel.shape[0])
            early = utter, conv_gain[None, :], bn_scale[None, :], bn_shift[None, :]
            mid_own, mid_full, early = grouped_ffn(tokens, ffn_gain, w_in, w_out, early)
            return grouped_conv_module(
                mid_own, mid_full, tok, early, w_value, w_gate, depth_kernel, w_proj
            )
        mid_own, mid_full = gathered_ffn(tokens, ffn_gain, w_in, w_out)
        return conv_module(mid_own, mid_full, tok, conv_gain, *rest)

    placed = (
        P(tok, "hid"),
        P(),
        P(tok, "hid"),
        P("hid", tok),
        P(),
        P(None, "hid"),
        P(None, "hid"),
        P(None, "hid"),
        P("hid"),
        P("hid"),
        P(None, "hid"),
        P(),
    )
    return jax.shard_map(
        local, mesh=inner, in_specs=placed, out_specs=P(tok, "hid"), check_vma=False
    )
```

```python
import functools

import jax
import jax.numpy as jnp
from jax import lax
from jax.experimental import pallas as pl
from jax.experimental.pallas import tpu as pltpu
from jax.sharding import Mesh, PartitionSpec as P

SWAP = [(0, 1), (1, 0)]


def norm_rows(values, gain):
    mean = jnp.mean(values, axis=-1, keepdims=True)
    centred = values - mean
    var = jnp.mean(centred * centred, axis=-1, keepdims=True)
    return centred * lax.rsqrt(var + 1e-05) * gain


def padded(cells, axis, width):
    count = lax.axis_size(axis)
    ends = count - 1
    head = cells[:width]
    tail = cells[cells.shape[0] - width :]
    return jnp.concatenate(
        [
            lax.ppermute(tail, axis, [(i, (i + 1) % count) for i in range(ends)]),
            cells,
            lax.ppermute(head, axis, [((i + 1) % count, i) for i in range(ends)]),
        ],
        axis=0,
    )


def conv_module(mid_own, mid_full, axis, conv_gain, w_value, w_gate, depth_kernel, bn_scale, bn_shift, w_proj, lengths):
    rows, width = mid_own.shape
    mid_normed = norm_rows(mid_full.astype(jnp.float32), conv_gain).astype(jnp.bfloat16)
    value = jnp.dot(mid_normed, w_value, preferred_element_type=jnp.float32)
    gate = jnp.dot(mid_normed, w_gate, preferred_element_type=jnp.float32)
    glu = (value * jax.nn.sigmoid(gate)).astype(jnp.bfloat16)
    extended = padded(glu, axis, 16).astype(jnp.float32)
    ends = jnp.cumsum(lengths)
    first_row = lax.axis_index(axis) * rows - 16
    positions = first_row + jnp.arange(rows + 32, dtype=jnp.int32)
    utter = jnp.sum((ends[None, :] <= positions[:, None]).astype(jnp.int32), axis=1)
    centre = utter[16 : 16 + rows]
    conv = jnp.zeros((rows, width), jnp.float32)
    for tap in range(depth_kernel.shape[0]):
        same = (utter[tap + 1 : tap + 1 + rows] == centre)[:, None]
        conv = conv + jnp.where(
            same, extended[tap + 1 : tap + 1 + rows] * depth_kernel[tap][None, :], 0.0
        )
    act = jax.nn.silu(conv * bn_scale + bn_shift).astype(jnp.bfloat16)
    act_full = lax.all_gather(act, "hid", axis=1, tiled=True)
    projected = jnp.dot(act_full, w_proj, preferred_element_type=jnp.float32)
    return (mid_own.astype(jnp.float32) + projected).astype(jnp.bfloat16)


def gathered_ffn(tokens, ffn_gain, w_in, w_out):
    whole = lax.all_gather(tokens, "hid", axis=1, tiled=True)
    normed = norm_rows(whole.astype(jnp.float32), ffn_gain).astype(jnp.bfloat16)
    pre = jnp.dot(
        normed, lax.all_gather(w_in, "tok", axis=0, tiled=True), preferred_element_type=jnp.float32
    )
    hidden = jax.nn.silu(pre).astype(jnp.bfloat16)
    partial_sum = jnp.dot(
        hidden, lax.all_gather(w_out, "tok", axis=1, tiled=True), preferred_element_type=jnp.float32
    )
    share = lax.psum_scatter(
        partial_sum.astype(jnp.bfloat16), "hid", scatter_dimension=1, tiled=True
    ).astype(jnp.float32)
    mid_own = (tokens.astype(jnp.float32) + 0.5 * share).astype(jnp.bfloat16)
    return mid_own, lax.all_gather(mid_own, "hid", axis=1, tiled=True)


GROUP = ("bh", "bl")
VMEM_LIMIT = 40 * 2**20
VMEM = pl.BlockSpec(memory_space=pltpu.VMEM)
SMEM = pl.BlockSpec(memory_space=pltpu.SMEM)


def kernel_call(body, outs, ins, scratch=(), scalars=0, flops=0, moved=0):
    return pl.pallas_call(
        body,
        out_shape=[jax.ShapeDtypeStruct(shape, dtype) for shape, dtype in outs],
        in_specs=[SMEM] * scalars + [VMEM] * (len(ins) - scalars),
        out_specs=[VMEM] * len(outs),
        scratch_shapes=list(scratch),
        compiler_params=pltpu.CompilerParams(vmem_limit_bytes=VMEM_LIMIT),
        cost_estimate=pl.CostEstimate(flops=flops, bytes_accessed=moved, transcendentals=0),
    )(*ins)


def f32(values):
    return values.astype(jnp.float32)


def silu(values):
    return values / (1.0 + jnp.exp(-values))


def cut_kernel(*refs):
    *arrays, out_ref = refs
    parts, _, width = out_ref.shape
    for part in range(parts):
        at = 0
        for ref in arrays:
            rows = ref.shape[0]
            out_ref[part, at : at + rows, :] = ref[:, part * width : (part + 1) * width]
            at += rows


def part_kernel(both_ref, first_ref, second_ref):
    half, shard, _ = first_ref.shape
    skip = both_ref.shape[1] - shard
    first_ref[...] = both_ref[:half, skip:, :]
    second_ref[...] = both_ref[half:, skip:, :]


def norm_kernel(me_ref, whole_ref, gain_ref, near_ref, far_ref, out_ref, upper_ref, lower_ref):
    rows, width = near_ref.shape
    at = pl.ds(pl.multiple_of(me_ref[1] * rows, rows), rows)
    for place, ref in ((me_ref[2], near_ref), (1 - me_ref[2], far_ref)):
        ref[...] = whole_ref[at, pl.ds(pl.multiple_of(place * width, width), width)]
    normed = norm_rows(f32(whole_ref[at, :]), gain_ref[...]).astype(jnp.bfloat16)
    out_ref[...] = normed
    upper_ref[...] = normed[: rows // 2]
    lower_ref[...] = normed[rows // 2 :]


def join_kernel(*refs):
    *pieces, out_ref = refs
    at = 0
    for piece in pieces:
        out_ref[at : at + piece.shape[0]] = piece[...]
        at += piece.shape[0]


def interleave(full_ref, base, block, own_refs, other_refs, me_l, last=False):
    for refs, turn in ((own_refs, me_l), (other_refs, 1 - me_l)):
        blocks = [(ref, j) for ref in refs for j in range(ref.shape[0])]
        for i, (ref, j) in enumerate(blocks):
            at = pl.multiple_of(base + (2 * i + turn) * block, block)
            skip = ref.shape[1] - block if last else 0
            full_ref[pl.ds(at, block), :] = ref[j, skip : skip + block, :]


def hidden_kernel(me_ref, x_ref, both_ref, both_x_ref, z_ref, zx_ref, h_ref, w_ref):
    me_l, me_a = me_ref[0], me_ref[2]
    part, block = w_ref.shape[0] // 2, z_ref.shape[1]
    interleave(w_ref, me_a * part, block, [both_ref], [both_x_ref], me_l)
    interleave(w_ref, (1 - me_a) * part, block, [z_ref], [zx_ref], me_l)
    step = 256
    for at in range(0, x_ref.shape[0], step):
        pre = jnp.dot(x_ref[at : at + step, :], w_ref[...], preferred_element_type=jnp.float32)
        h_ref[at : at + step, :] = silu(pre).astype(jnp.bfloat16)


def sums_kernel(n_own, me_ref, own_ref, oth_ref, *refs):
    *blocks, kept_ref, sent_ref, w_ref = refs
    block = w_ref.shape[0] // 8
    interleave(w_ref, 0, block, blocks[:n_own], blocks[n_own:], me_ref[0], True)
    step = 256
    for h_ref, out_ref in ((oth_ref, sent_ref), (own_ref, kept_ref)):
        for at in range(0, h_ref.shape[0], step):
            out_ref[at : at + step, :] = lax.dot_general(
                h_ref[at : at + step, :],
                w_ref[...],
                (((1,), (1,)), ((), ())),
                preferred_element_type=jnp.float32,
            ).astype(out_ref.dtype)


def add_kernel(kept_ref, came_ref, *out_refs):
    rows = out_refs[0].shape[0]
    for k, out_ref in enumerate(out_refs):
        at = slice(k * rows, (k + 1) * rows)
        out_ref[...] = (kept_ref[at, :] + f32(came_ref[at, :])).astype(out_ref.dtype)


def mid_kernel(mine_ref, first_ref, *refs):
    *others, out_ref = refs
    total = first_ref[...]
    for other in others:
        total = total + f32(other[...])
    out_ref[...] = (f32(mine_ref[...]) + 0.5 * total).astype(jnp.bfloat16)


HALO = 16


def utter_kernel(first_ref, lengths_ref, out_ref, base_ref):
    position = first_ref[0] + lax.broadcasted_iota(jnp.int32, base_ref.shape, 0)

    def step(u, carry):
        end, utter = carry
        end = end + lengths_ref[u]
        return end, utter + jnp.where(position >= end, 1, 0)

    zero = jnp.zeros(base_ref.shape, jnp.int32)
    base_ref[...] = lax.fori_loop(0, lengths_ref.shape[0], step, (jnp.int32(0), zero))[1]
    for r in range(8):
        out_ref[r] = base_ref[1 + r : 1 + r + out_ref.shape[1], :]


def glu_kernel(
    me_ref, near_ref, near_oth_ref, far_ref, far_oth_ref, gain_ref, value_ref, gate_ref,
    glu_ref, head_ref, tail_ref, own_ref, mid_ref
):
    rows, width = near_ref.shape
    me_c, me_a = me_ref[1], me_ref[2]
    for core, near, far in ((me_c, near_ref, far_ref), (1 - me_c, near_oth_ref, far_oth_ref)):
        at = pl.ds(pl.multiple_of(core * rows, rows), rows)
        for place, ref in ((me_a, near), (1 - me_a, far)):
            mid_ref[at, pl.ds(pl.multiple_of(place * width, width), width)] = ref[...]
    own_ref[...] = mid_ref[:, pl.ds(pl.multiple_of(me_c * width, width), width)]
    normed = norm_rows(f32(mid_ref[...]), gain_ref[...]).astype(jnp.bfloat16)
    value = jnp.dot(normed, value_ref[...], preferred_element_type=jnp.float32)
    gate = jnp.dot(normed, gate_ref[...], preferred_element_type=jnp.float32)
    glu = (value / (1.0 + jnp.exp(-gate))).astype(jnp.bfloat16)
    glu_ref[...] = glu
    head_ref[...] = glu[:HALO]
    tail_ref[...] = glu[glu.shape[0] - HALO :]


def conv_rows(ext_ref, utter_ref, taps_ref, scale_ref, shift_ref, out_ref, tiles, step):
    width = out_ref.shape[1]
    taps = taps_ref.shape[0]
    lanes = 128
    group = 3 if width % (3 * lanes) == 0 else 1
    span = step + taps - 8

    def columns(i, _):
        at_lane = [pl.ds(pl.multiple_of((i * group + g) * lanes, lanes), lanes) for g in range(group)]
        for ext_at, at, out_at in tiles:
            centre = utter_ref[7, at + HALO - 8 : at + HALO - 8 + step, :]
            totals = [jnp.zeros((step, lanes), jnp.float32)] * group
            for r in range(8):
                cells = [ext_ref[ext_at + 1 + r : ext_at + 1 + r + span, c] for c in at_lane]
                for q in range(0, taps, 8):
                    same = utter_ref[r, at + q : at + q + step, :] == centre
                    for g, c in enumerate(at_lane):
                        term = cells[g][q : q + step] * taps_ref[q + r : q + r + 1, c]
                        totals[g] = totals[g] + jnp.where(same, term, 0.0)
            for total, c in zip(totals, at_lane):
                act = silu(total * scale_ref[:, c] + shift_ref[:, c])
                out_ref[out_at : out_at + step, c] = act.astype(out_ref.dtype)
        return 0

    lax.fori_loop(0, width // (group * lanes), columns, 0)


def inner_conv_kernel(glu_ref, utter_ref, taps_ref, scale_ref, shift_ref, out_ref, ext_ref):
    ext_ref[...] = f32(glu_ref[...])
    step = 2 * HALO
    tiles = [(at - HALO, at, at) for at in range(HALO, out_ref.shape[0] - HALO, step)]
    conv_rows(ext_ref, utter_ref, taps_ref, scale_ref, shift_ref, out_ref, tiles, step)


def edge_conv_kernel(
    act_ref, top_ref, glu_ref, bottom_ref, utter_ref, taps_ref, scale_ref, shift_ref, out_ref, ext_ref
):
    rows = out_ref.shape[0]
    last = rows - HALO
    out_ref[HALO:last, :] = act_ref[HALO:last, :]
    ext_ref[:HALO, :] = f32(top_ref[...])
    ext_ref[HALO : 3 * HALO, :] = f32(glu_ref[: 2 * HALO, :])
    ext_ref[3 * HALO : 5 * HALO, :] = f32(glu_ref[rows - 2 * HALO :, :])
    ext_ref[5 * HALO :, :] = f32(bottom_ref[...])
    tiles = [(0, 0, 0), (3 * HALO, last, last)]
    conv_rows(ext_ref, utter_ref, taps_ref, scale_ref, shift_ref, out_ref, tiles, HALO)


def utterances(rows, axis, lengths, taps):
    return kernel_call(
        utter_kernel,
        [((8, rows + taps - 8, 128), jnp.int32)],
        [(lax.axis_index(axis) * rows - HALO)[None], lengths],
        scratch=[pltpu.VMEM((rows + 2 * HALO, 128), jnp.int32)],
        scalars=2,
    )[0]


def grouped_conv_module(mid, me, axis, early, w_value, w_gate, depth_kernel, w_proj):
    half, width = mid[0].shape
    rows = 2 * half
    utter, conv_gain, bn_scale, bn_shift = early
    bf16 = jnp.bfloat16
    glu, head, tail, mid_own = kernel_call(
        glu_kernel,
        [((rows, width), bf16)] + [((HALO, width), bf16)] * 2 + [((rows, width), bf16)],
        [me, *mid, conv_gain, w_value, w_gate],
        scratch=[pltpu.VMEM((rows, 2 * width), bf16)],
        scalars=1,
        flops=4 * rows * w_value.size,
        moved=4 * w_value.size,
    )
    count = lax.axis_size(axis)
    top = lax.ppermute(tail, axis, [(i, i + 1) for i in range(count - 1)])
    bottom = lax.ppermute(head, axis, [(i + 1, i) for i in range(count - 1)])
    rest = [utter, depth_kernel, bn_scale, bn_shift]
    (act,) = kernel_call(
        inner_conv_kernel,
        [((rows, width), bf16)],
        [glu, *rest],
        scratch=[pltpu.VMEM((rows, width), jnp.float32)],
        flops=rows * depth_kernel.size,
        moved=16 * rows * width,
    )
    (act,) = kernel_call(
        edge_conv_kernel,
        [((rows, width), bf16)],
        [act, top, glu, bottom, *rest],
        scratch=[pltpu.VMEM((6 * HALO, width), jnp.float32)],
        flops=HALO * depth_kernel.size,
        moved=4 * rows * width,
    )
    act_full = lax.all_gather(act, "hid", axis=1, tiled=True)
    projected = jnp.dot(act_full, w_proj, preferred_element_type=jnp.float32)
    return (mid_own.astype(jnp.float32) + projected).astype(jnp.bfloat16)


def partner(values, step):
    return lax.ppermute(values, GROUP, [(i, i ^ step) for i in range(4)])


def swap(values, axis):
    return lax.ppermute(values, axis, SWAP)


def recut(parts):
    return lax.all_to_all(parts, GROUP, 0, 0)


def grouped_ffn(tokens, ffn_gain, w_in, w_out, early):
    rows, width = tokens.shape
    half = rows // 2
    shard, hid = w_in.shape
    wide = 2 * width
    units = hid // 4
    bf16 = jnp.bfloat16
    me_c = lax.axis_index("hid")
    me = jnp.stack([lax.axis_index("al"), me_c, lax.axis_index("ah")])
    tie = lax.optimization_barrier

    block, pair = (4, shard, units), (2, shard, units)
    in_far = swap(w_in, "ah")
    (both,) = kernel_call(cut_kernel, [((4, 2 * shard, units), bf16)], [w_in, w_out.T])
    both = recut(both)
    whole = lax.all_gather(tokens, "hid", axis=1, tiled=True)
    *mine, normed, upper, lower = kernel_call(
        norm_kernel,
        [((half, width), bf16)] * 2 + [((half, wide), bf16)] + [((half // 2, wide), bf16)] * 2,
        [me, whole, ffn_gain[None, :]],
        scalars=1,
    )
    frames1 = partner(normed, 1)
    in_far, both, normed, upper, lower, frames1, early = tie(
        (in_far, both, normed, upper, lower, frames1, early)
    )
    both_x = swap(both, "al")
    (in_z,) = kernel_call(cut_kernel, [(block, bf16)], [in_far])
    in_z = recut(in_z)
    out_1, out_2 = kernel_call(part_kernel, [(pair, bf16)] * 2, [both])
    out_z1 = swap(out_1, "ah")
    frames3 = partner(normed, 3)
    both_x, in_z, out_z1, out_2 = tie((both_x, in_z, out_z1, out_2))
    in_zx = swap(in_z, "al")
    out_z2 = swap(out_2, "ah")
    normed, upper, lower, frames3 = tie((normed, upper, lower, frames3))
    frames2 = [partner(upper, 2), partner(lower, 2)]
    in_zx, out_z1, out_z2, frames2 = tie((in_zx, out_z1, out_z2, frames2))
    out_zx1 = swap(out_z1, "al")
    out_zx2 = swap(out_z2, "al")
    (x_own,) = kernel_call(
        join_kernel, [((4 * half, wide), bf16)], [normed, frames1, *frames2, frames3]
    )
    x_oth = swap(x_own, "hid")

    def units_of(x):
        return kernel_call(
            hidden_kernel,
            [((4 * half, units), bf16)],
            [me, x, both, both_x, in_z, in_zx],
            scratch=[pltpu.VMEM((wide, units), bf16)],
            scalars=1,
        )[0]

    hidden = [units_of(x_own), units_of(x_oth)]

    def products(own, other):
        return kernel_call(
            functools.partial(sums_kernel, len(own)),
            [((4 * half, width), jnp.float32), ((4 * half, width), bf16)],
            [me, *hidden, *own, *other],
            scratch=[pltpu.VMEM((width, units), bf16)],
            scalars=1,
        )

    def scatter(kept, sent):
        total = kernel_call(
            add_kernel,
            [((half, width), jnp.float32)] + [((half, width), bf16)] * 3,
            [kept, swap(sent, "hid")],
        )
        return [total[0]] + [partner(v, k + 1) for k, v in enumerate(total[1:])]

    near, out_zx1, out_zx2 = tie((products([both], [both_x]), out_zx1, out_zx2))
    far = products([out_z1, out_z2], [out_zx1, out_zx2])
    mine_near, mine_far = mine

    def mid(rows, parts):
        (own,) = kernel_call(mid_kernel, [((half, width), bf16)], [rows, *parts])
        return own, swap(own, "hid")

    near, parts = tie((mid(mine_near, scatter(*near)), scatter(*far)))
    return near + mid(mine_far, parts), me, early


def solution(mesh):
    n_tok, n_hid = mesh.shape["tok"], mesh.shape["hid"]
    grouped = n_tok == 16 and n_hid == 2
    if grouped:
        tok = ("ah", "bh", "bl", "al")
        inner = Mesh(mesh.devices.reshape(2, 2, 2, 2, n_hid), tok + ("hid",))
    else:
        tok, inner = "tok", mesh

    def local(tokens, ffn_gain, w_in, w_out, conv_gain, *rest):
        if grouped:
            w_value, w_gate, depth_kernel, bn_scale, bn_shift, w_proj, lengths = rest
            utter = utterances(tokens.shape[0], tok, lengths, depth_kernel.shape[0])
            early = utter, conv_gain[None, :], bn_scale[None, :], bn_shift[None, :]
            mid, me, early = grouped_ffn(tokens, ffn_gain, w_in, w_out, early)
            return grouped_conv_module(mid, me, tok, early, w_value, w_gate, depth_kernel, w_proj)
        mid_own, mid_full = gathered_ffn(tokens, ffn_gain, w_in, w_out)
        return conv_module(mid_own, mid_full, tok, conv_gain, *rest)

    placed = (
        P(tok, "hid"),
        P(),
        P(tok, "hid"),
        P("hid", tok),
        P(),
        P(None, "hid"),
        P(None, "hid"),
        P(None, "hid"),
        P("hid"),
        P("hid"),
        P(None, "hid"),
        P(),
    )
    return jax.shard_map(
        local, mesh=inner, in_specs=placed, out_specs=P(tok, "hid"), check_vma=False
    )
```

```python
import functools

import jax
import jax.numpy as jnp
from jax import lax
from jax.experimental import pallas as pl
from jax.experimental.pallas import tpu as pltpu
from jax.sharding import Mesh, PartitionSpec as P

SWAP = [(0, 1), (1, 0)]


def norm_rows(values, gain):
    mean = jnp.mean(values, axis=-1, keepdims=True)
    centred = values - mean
    var = jnp.mean(centred * centred, axis=-1, keepdims=True)
    return centred * lax.rsqrt(var + 1e-05) * gain


def padded(cells, axis, width):
    count = lax.axis_size(axis)
    ends = count - 1
    head = cells[:width]
    tail = cells[cells.shape[0] - width :]
    return jnp.concatenate(
        [
            lax.ppermute(tail, axis, [(i, (i + 1) % count) for i in range(ends)]),
            cells,
            lax.ppermute(head, axis, [((i + 1) % count, i) for i in range(ends)]),
        ],
        axis=0,
    )


def conv_module(mid_own, mid_full, axis, conv_gain, w_value, w_gate, depth_kernel, bn_scale, bn_shift, w_proj, lengths):
    rows, width = mid_own.shape
    mid_normed = norm_rows(mid_full.astype(jnp.float32), conv_gain).astype(jnp.bfloat16)
    value = jnp.dot(mid_normed, w_value, preferred_element_type=jnp.float32)
    gate = jnp.dot(mid_normed, w_gate, preferred_element_type=jnp.float32)
    glu = (value * jax.nn.sigmoid(gate)).astype(jnp.bfloat16)
    extended = padded(glu, axis, 16).astype(jnp.float32)
    ends = jnp.cumsum(lengths)
    first_row = lax.axis_index(axis) * rows - 16
    positions = first_row + jnp.arange(rows + 32, dtype=jnp.int32)
    utter = jnp.sum((ends[None, :] <= positions[:, None]).astype(jnp.int32), axis=1)
    centre = utter[16 : 16 + rows]
    conv = jnp.zeros((rows, width), jnp.float32)
    for tap in range(depth_kernel.shape[0]):
        same = (utter[tap + 1 : tap + 1 + rows] == centre)[:, None]
        conv = conv + jnp.where(
            same, extended[tap + 1 : tap + 1 + rows] * depth_kernel[tap][None, :], 0.0
        )
    act = jax.nn.silu(conv * bn_scale + bn_shift).astype(jnp.bfloat16)
    act_full = lax.all_gather(act, "hid", axis=1, tiled=True)
    projected = jnp.dot(act_full, w_proj, preferred_element_type=jnp.float32)
    return (mid_own.astype(jnp.float32) + projected).astype(jnp.bfloat16)


def gathered_ffn(tokens, ffn_gain, w_in, w_out):
    whole = lax.all_gather(tokens, "hid", axis=1, tiled=True)
    normed = norm_rows(whole.astype(jnp.float32), ffn_gain).astype(jnp.bfloat16)
    pre = jnp.dot(
        normed, lax.all_gather(w_in, "tok", axis=0, tiled=True), preferred_element_type=jnp.float32
    )
    hidden = jax.nn.silu(pre).astype(jnp.bfloat16)
    partial_sum = jnp.dot(
        hidden, lax.all_gather(w_out, "tok", axis=1, tiled=True), preferred_element_type=jnp.float32
    )
    share = lax.psum_scatter(
        partial_sum.astype(jnp.bfloat16), "hid", scatter_dimension=1, tiled=True
    ).astype(jnp.float32)
    mid_own = (tokens.astype(jnp.float32) + 0.5 * share).astype(jnp.bfloat16)
    return mid_own, lax.all_gather(mid_own, "hid", axis=1, tiled=True)


GROUP = ("bh", "bl")
VMEM = pl.BlockSpec(memory_space=pltpu.VMEM)
SMEM = pl.BlockSpec(memory_space=pltpu.SMEM)


def kernel_call(body, outs, ins, scratch=(), scalars=0, flops=0, moved=0, limit=40):
    return pl.pallas_call(
        body,
        out_shape=[jax.ShapeDtypeStruct(shape, dtype) for shape, dtype in outs],
        in_specs=[SMEM] * scalars + [VMEM] * (len(ins) - scalars),
        out_specs=[VMEM] * len(outs),
        scratch_shapes=list(scratch),
        compiler_params=pltpu.CompilerParams(vmem_limit_bytes=limit * 2**20),
        cost_estimate=pl.CostEstimate(flops=flops, bytes_accessed=moved, transcendentals=0),
    )(*ins)


def f32(values):
    return values.astype(jnp.float32)


def silu(values):
    return values / (1.0 + jnp.exp(-values))


def cut_kernel(*refs):
    *arrays, out_ref = refs
    parts, _, width = out_ref.shape
    for part in range(parts):
        at = 0
        for ref in arrays:
            rows = ref.shape[0]
            out_ref[part, at : at + rows, :] = ref[:, part * width : (part + 1) * width]
            at += rows


def part_kernel(both_ref, first_ref, second_ref):
    half, shard, _ = first_ref.shape
    skip = both_ref.shape[1] - shard
    first_ref[...] = both_ref[:half, skip:, :]
    second_ref[...] = both_ref[half:, skip:, :]


def norm_kernel(me_ref, whole_ref, gain_ref, near_ref, far_ref, out_ref):
    rows, width = near_ref.shape
    at = pl.ds(pl.multiple_of(me_ref[1] * rows, rows), rows)
    for place, ref in ((me_ref[2], near_ref), (1 - me_ref[2], far_ref)):
        ref[...] = whole_ref[at, pl.ds(pl.multiple_of(place * width, width), width)]
    out_ref[...] = norm_rows(f32(whole_ref[at, :]), gain_ref[...]).astype(jnp.bfloat16)


def part_rows_kernel(ref, first_ref, second_ref):
    half = first_ref.shape[0]
    first_ref[...] = ref[:half]
    second_ref[...] = ref[half:]


def interleave(full_ref, base, block, own_refs, other_refs, me_l, last=False):
    for refs, turn in ((own_refs, me_l), (other_refs, 1 - me_l)):
        blocks = [(ref, j) for ref in refs for j in range(ref.shape[0])]
        for i, (ref, j) in enumerate(blocks):
            at = pl.multiple_of(base + (2 * i + turn) * block, block)
            skip = ref.shape[1] - block if last else 0
            full_ref[pl.ds(at, block), :] = ref[j, skip : skip + block, :]


def hidden_kernel(n_x, me_ref, *refs):
    pieces, (both_ref, both_x_ref, z_ref, zx_ref, h_ref, w_ref, x_ref) = refs[:n_x], refs[n_x:]
    me_l, me_a = me_ref[0], me_ref[2]
    part, block = w_ref.shape[0] // 2, z_ref.shape[1]
    interleave(w_ref, me_a * part, block, [both_ref], [both_x_ref], me_l)
    interleave(w_ref, (1 - me_a) * part, block, [z_ref], [zx_ref], me_l)
    at = 0
    for piece in pieces:
        x_ref[at : at + piece.shape[0], :] = piece[...]
        at += piece.shape[0]
    step = 256
    for at in range(0, x_ref.shape[0], step):
        pre = jnp.dot(x_ref[at : at + step, :], w_ref[...], preferred_element_type=jnp.float32)
        h_ref[at : at + step, :] = silu(pre).astype(jnp.bfloat16)


def sums_kernel(n_own, me_ref, own_ref, oth_ref, *refs):
    *blocks, kept_ref, sent_ref, w_ref = refs
    block = w_ref.shape[0] // 8
    interleave(w_ref, 0, block, blocks[:n_own], blocks[n_own:], me_ref[0], True)
    step = 256
    for h_ref, out_ref in ((oth_ref, sent_ref), (own_ref, kept_ref)):
        for at in range(0, h_ref.shape[0], step):
            out_ref[at : at + step, :] = lax.dot_general(
                h_ref[at : at + step, :],
                w_ref[...],
                (((1,), (1,)), ((), ())),
                preferred_element_type=jnp.float32,
            ).astype(out_ref.dtype)


def add_kernel(kept_ref, came_ref, *out_refs):
    rows = out_refs[0].shape[0]
    for k, out_ref in enumerate(out_refs):
        at = slice(k * rows, (k + 1) * rows)
        out_ref[...] = (kept_ref[at, :] + f32(came_ref[at, :])).astype(out_ref.dtype)


def mid_kernel(mine_ref, first_ref, *refs):
    *others, out_ref = refs
    total = first_ref[...]
    for other in others:
        total = total + f32(other[...])
    out_ref[...] = (f32(mine_ref[...]) + 0.5 * total).astype(jnp.bfloat16)


HALO = 16


def utter_kernel(first_ref, lengths_ref, out_ref, base_ref):
    position = first_ref[0] + lax.broadcasted_iota(jnp.int32, base_ref.shape, 0)

    def step(u, carry):
        end, utter = carry
        end = end + lengths_ref[u]
        return end, utter + jnp.where(position >= end, 1, 0)

    zero = jnp.zeros(base_ref.shape, jnp.int32)
    base_ref[...] = lax.fori_loop(0, lengths_ref.shape[0], step, (jnp.int32(0), zero))[1]
    for r in range(8):
        out_ref[r] = base_ref[1 + r : 1 + r + out_ref.shape[1], :]


def glu_kernel(
    me_ref, near_ref, near_oth_ref, far_ref, far_oth_ref, gain_ref, value_ref, gate_ref,
    glu_ref, head_ref, tail_ref, own_ref, mid_ref
):
    rows, width = near_ref.shape
    me_c, me_a = me_ref[1], me_ref[2]
    for core, near, far in ((me_c, near_ref, far_ref), (1 - me_c, near_oth_ref, far_oth_ref)):
        at = pl.ds(pl.multiple_of(core * rows, rows), rows)
        for place, ref in ((me_a, near), (1 - me_a, far)):
            mid_ref[at, pl.ds(pl.multiple_of(place * width, width), width)] = ref[...]
    own_ref[...] = mid_ref[:, pl.ds(pl.multiple_of(me_c * width, width), width)]
    normed = norm_rows(f32(mid_ref[...]), gain_ref[...]).astype(jnp.bfloat16)
    value = jnp.dot(normed, value_ref[...], preferred_element_type=jnp.float32)
    gate = jnp.dot(normed, gate_ref[...], preferred_element_type=jnp.float32)
    glu = (value / (1.0 + jnp.exp(-gate))).astype(jnp.bfloat16)
    glu_ref[...] = glu
    head_ref[...] = glu[:HALO]
    tail_ref[...] = glu[glu.shape[0] - HALO :]


def conv_rows(ext_ref, utter_ref, taps_ref, scale_ref, shift_ref, out_ref, tiles, step):
    width = out_ref.shape[1]
    taps = taps_ref.shape[0]
    lanes = 128
    group = 3 if width % (3 * lanes) == 0 else 1
    span = step + taps - 8

    def columns(i, _):
        at_lane = [pl.ds(pl.multiple_of((i * group + g) * lanes, lanes), lanes) for g in range(group)]
        for ext_at, at, out_at in tiles:
            centre = utter_ref[7, at + HALO - 8 : at + HALO - 8 + step, :]
            totals = [jnp.zeros((step, lanes), jnp.float32)] * group
            for r in range(8):
                cells = [ext_ref[ext_at + 1 + r : ext_at + 1 + r + span, c] for c in at_lane]
                for q in range(0, taps, 8):
                    same = utter_ref[r, at + q : at + q + step, :] == centre
                    for g, c in enumerate(at_lane):
                        term = cells[g][q : q + step] * taps_ref[q + r : q + r + 1, c]
                        totals[g] = totals[g] + jnp.where(same, term, 0.0)
            for total, c in zip(totals, at_lane):
                act = silu(total * scale_ref[:, c] + shift_ref[:, c])
                out_ref[out_at : out_at + step, c] = act.astype(out_ref.dtype)
        return 0

    lax.fori_loop(0, width // (group * lanes), columns, 0)


def inner_conv_kernel(glu_ref, utter_ref, taps_ref, scale_ref, shift_ref, out_ref, ext_ref):
    ext_ref[...] = f32(glu_ref[...])
    step = 2 * HALO
    tiles = [(at - HALO, at, at) for at in range(HALO, out_ref.shape[0] - HALO, step)]
    conv_rows(ext_ref, utter_ref, taps_ref, scale_ref, shift_ref, out_ref, tiles, step)


def edge_conv_kernel(
    act_ref, top_ref, glu_ref, bottom_ref, utter_ref, taps_ref, scale_ref, shift_ref, out_ref, ext_ref
):
    rows = out_ref.shape[0]
    last = rows - HALO
    out_ref[HALO:last, :] = act_ref[HALO:last, :]
    ext_ref[:HALO, :] = f32(top_ref[...])
    ext_ref[HALO : 3 * HALO, :] = f32(glu_ref[: 2 * HALO, :])
    ext_ref[3 * HALO : 5 * HALO, :] = f32(glu_ref[rows - 2 * HALO :, :])
    ext_ref[5 * HALO :, :] = f32(bottom_ref[...])
    tiles = [(0, 0, 0), (3 * HALO, last, last)]
    conv_rows(ext_ref, utter_ref, taps_ref, scale_ref, shift_ref, out_ref, tiles, HALO)


def utterances(rows, axis, lengths, taps):
    return kernel_call(
        utter_kernel,
        [((8, rows + taps - 8, 128), jnp.int32)],
        [(lax.axis_index(axis) * rows - HALO)[None], lengths],
        scratch=[pltpu.VMEM((rows + 2 * HALO, 128), jnp.int32)],
        scalars=2,
    )[0]


def grouped_conv_module(mid, me, axis, early, w_value, w_gate, depth_kernel, w_proj):
    half, width = mid[0].shape
    rows = 2 * half
    utter, conv_gain, bn_scale, bn_shift = early
    bf16 = jnp.bfloat16
    glu, head, tail, mid_own = kernel_call(
        glu_kernel,
        [((rows, width), bf16)] + [((HALO, width), bf16)] * 2 + [((rows, width), bf16)],
        [me, *mid, conv_gain, w_value, w_gate],
        scratch=[pltpu.VMEM((rows, 2 * width), bf16)],
        scalars=1,
        flops=4 * rows * w_value.size,
        moved=4 * w_value.size,
    )
    count = lax.axis_size(axis)
    top = lax.ppermute(tail, axis, [(i, i + 1) for i in range(count - 1)])
    bottom = lax.ppermute(head, axis, [(i + 1, i) for i in range(count - 1)])
    rest = [utter, depth_kernel, bn_scale, bn_shift]
    (act,) = kernel_call(
        inner_conv_kernel,
        [((rows, width), bf16)],
        [glu, *rest],
        scratch=[pltpu.VMEM((rows, width), jnp.float32)],
        flops=rows * depth_kernel.size,
        moved=16 * rows * width,
    )
    (act,) = kernel_call(
        edge_conv_kernel,
        [((rows, width), bf16)],
        [act, top, glu, bottom, *rest],
        scratch=[pltpu.VMEM((6 * HALO, width), jnp.float32)],
        flops=HALO * depth_kernel.size,
        moved=4 * rows * width,
    )
    act_full = lax.all_gather(act, "hid", axis=1, tiled=True)
    projected = jnp.dot(act_full, w_proj, preferred_element_type=jnp.float32)
    return (mid_own.astype(jnp.float32) + projected).astype(jnp.bfloat16)


def partner(values, step):
    return lax.ppermute(values, GROUP, [(i, i ^ step) for i in range(4)])


def swap(values, axis):
    return lax.ppermute(values, axis, SWAP)


def recut(parts):
    return lax.all_to_all(parts, GROUP, 0, 0)


def grouped_ffn(tokens, ffn_gain, w_in, w_out, early):
    rows, width = tokens.shape
    half = rows // 2
    shard, hid = w_in.shape
    wide = 2 * width
    units = hid // 4
    bf16 = jnp.bfloat16
    me_c = lax.axis_index("hid")
    me = jnp.stack([lax.axis_index("al"), me_c, lax.axis_index("ah")])
    tie = lax.optimization_barrier

    block, pair = (4, shard, units), (2, shard, units)
    in_far = swap(w_in, "ah")
    (both,) = kernel_call(cut_kernel, [((4, 2 * shard, units), bf16)], [w_in, w_out.T], limit=60)
    both = recut(both)
    whole = lax.all_gather(tokens, "hid", axis=1, tiled=True)
    *mine, normed = kernel_call(
        norm_kernel,
        [((half, width), bf16)] * 2 + [((half, wide), bf16)],
        [me, whole, ffn_gain[None, :]],
        scalars=1,
    )
    frames1 = partner(normed, 1)
    in_far, both, normed, frames1, early = tie((in_far, both, normed, frames1, early))
    both_x = swap(both, "al")
    (in_z,) = kernel_call(cut_kernel, [(block, bf16)], [in_far])
    in_z = recut(in_z)
    out_1, out_2 = kernel_call(part_kernel, [(pair, bf16)] * 2, [both])
    out_z1 = swap(out_1, "ah")
    frames2 = partner(normed, 2)
    normed_oth, frames1_oth = swap(normed, "hid"), swap(frames1, "hid")
    both_x, in_z, out_z1, out_2, normed_oth, frames1_oth = tie(
        (both_x, in_z, out_z1, out_2, normed_oth, frames1_oth)
    )
    in_zx = swap(in_z, "al")
    out_z2 = swap(out_2, "ah")
    upper, lower = kernel_call(part_rows_kernel, [((half // 2, wide), bf16)] * 2, [frames2])
    frames3 = [partner(upper, 1), partner(lower, 1)]
    in_zx, out_z1, out_z2, frames3 = tie((in_zx, out_z1, out_z2, frames3))
    out_zx1 = swap(out_z1, "al")
    out_zx2 = swap(out_z2, "al")
    own = [normed, frames1, frames2, *frames3]
    others = [normed_oth, frames1_oth] + [swap(v, "hid") for v in own[2:]]

    def units_of(pieces):
        return kernel_call(
            functools.partial(hidden_kernel, len(pieces)),
            [((4 * half, units), bf16)],
            [me, *pieces, both, both_x, in_z, in_zx],
            scratch=[pltpu.VMEM((wide, units), bf16), pltpu.VMEM((4 * half, wide), bf16)],
            scalars=1,
        )[0]

    hidden = [units_of(own), units_of(others)]

    def products(own, other):
        return kernel_call(
            functools.partial(sums_kernel, len(own)),
            [((4 * half, width), jnp.float32), ((4 * half, width), bf16)],
            [me, *hidden, *own, *other],
            scratch=[pltpu.VMEM((width, units), bf16)],
            scalars=1,
        )

    def scatter(kept, sent):
        total = kernel_call(
            add_kernel,
            [((half, width), jnp.float32)] + [((half, width), bf16)] * 3,
            [kept, swap(sent, "hid")],
        )
        return [total[0]] + [partner(v, k + 1) for k, v in enumerate(total[1:])]

    near, out_zx1, out_zx2 = tie((products([both], [both_x]), out_zx1, out_zx2))
    far = products([out_z1, out_z2], [out_zx1, out_zx2])
    mine_near, mine_far = mine

    def mid(rows, parts):
        (own,) = kernel_call(mid_kernel, [((half, width), bf16)], [rows, *parts])
        return own, swap(own, "hid")

    near, parts = tie((mid(mine_near, scatter(*near)), scatter(*far)))
    return near + mid(mine_far, parts), me, early


def solution(mesh):
    n_tok, n_hid = mesh.shape["tok"], mesh.shape["hid"]
    grouped = n_tok == 16 and n_hid == 2
    if grouped:
        tok = ("ah", "bh", "bl", "al")
        inner = Mesh(mesh.devices.reshape(2, 2, 2, 2, n_hid), tok + ("hid",))
    else:
        tok, inner = "tok", mesh

    def local(tokens, ffn_gain, w_in, w_out, conv_gain, *rest):
        if grouped:
            w_value, w_gate, depth_kernel, bn_scale, bn_shift, w_proj, lengths = rest
            utter = utterances(tokens.shape[0], tok, lengths, depth_kernel.shape[0])
            early = utter, conv_gain[None, :], bn_scale[None, :], bn_shift[None, :]
            mid, me, early = grouped_ffn(tokens, ffn_gain, w_in, w_out, early)
            return grouped_conv_module(mid, me, tok, early, w_value, w_gate, depth_kernel, w_proj)
        mid_own, mid_full = gathered_ffn(tokens, ffn_gain, w_in, w_out)
        return conv_module(mid_own, mid_full, tok, conv_gain, *rest)

    placed = (
        P(tok, "hid"),
        P(),
        P(tok, "hid"),
        P("hid", tok),
        P(),
        P(None, "hid"),
        P(None, "hid"),
        P(None, "hid"),
        P("hid"),
        P("hid"),
        P(None, "hid"),
        P(),
    )
    return jax.shard_map(
        local, mesh=inner, in_specs=placed, out_specs=P(tok, "hid"), check_vma=False
    )
```

```python
import functools

import jax
import jax.numpy as jnp
from jax import lax
from jax.experimental import pallas as pl
from jax.experimental.pallas import tpu as pltpu
from jax.sharding import Mesh, PartitionSpec as P

SWAP = [(0, 1), (1, 0)]


def norm_rows(values, gain):
    mean = jnp.mean(values, axis=-1, keepdims=True)
    centred = values - mean
    var = jnp.mean(centred * centred, axis=-1, keepdims=True)
    return centred * lax.rsqrt(var + 1e-05) * gain


def padded(cells, axis, width):
    count = lax.axis_size(axis)
    ends = count - 1
    head = cells[:width]
    tail = cells[cells.shape[0] - width :]
    return jnp.concatenate(
        [
            lax.ppermute(tail, axis, [(i, (i + 1) % count) for i in range(ends)]),
            cells,
            lax.ppermute(head, axis, [((i + 1) % count, i) for i in range(ends)]),
        ],
        axis=0,
    )


def conv_module(mid_own, mid_full, axis, conv_gain, w_value, w_gate, depth_kernel, bn_scale, bn_shift, w_proj, lengths):
    rows, width = mid_own.shape
    mid_normed = norm_rows(mid_full.astype(jnp.float32), conv_gain).astype(jnp.bfloat16)
    value = jnp.dot(mid_normed, w_value, preferred_element_type=jnp.float32)
    gate = jnp.dot(mid_normed, w_gate, preferred_element_type=jnp.float32)
    glu = (value * jax.nn.sigmoid(gate)).astype(jnp.bfloat16)
    extended = padded(glu, axis, 16).astype(jnp.float32)
    ends = jnp.cumsum(lengths)
    first_row = lax.axis_index(axis) * rows - 16
    positions = first_row + jnp.arange(rows + 32, dtype=jnp.int32)
    utter = jnp.sum((ends[None, :] <= positions[:, None]).astype(jnp.int32), axis=1)
    centre = utter[16 : 16 + rows]
    conv = jnp.zeros((rows, width), jnp.float32)
    for tap in range(depth_kernel.shape[0]):
        same = (utter[tap + 1 : tap + 1 + rows] == centre)[:, None]
        conv = conv + jnp.where(
            same, extended[tap + 1 : tap + 1 + rows] * depth_kernel[tap][None, :], 0.0
        )
    act = jax.nn.silu(conv * bn_scale + bn_shift).astype(jnp.bfloat16)
    act_full = lax.all_gather(act, "hid", axis=1, tiled=True)
    projected = jnp.dot(act_full, w_proj, preferred_element_type=jnp.float32)
    return (mid_own.astype(jnp.float32) + projected).astype(jnp.bfloat16)


def gathered_ffn(tokens, ffn_gain, w_in, w_out):
    whole = lax.all_gather(tokens, "hid", axis=1, tiled=True)
    normed = norm_rows(whole.astype(jnp.float32), ffn_gain).astype(jnp.bfloat16)
    pre = jnp.dot(
        normed, lax.all_gather(w_in, "tok", axis=0, tiled=True), preferred_element_type=jnp.float32
    )
    hidden = jax.nn.silu(pre).astype(jnp.bfloat16)
    partial_sum = jnp.dot(
        hidden, lax.all_gather(w_out, "tok", axis=1, tiled=True), preferred_element_type=jnp.float32
    )
    share = lax.psum_scatter(
        partial_sum.astype(jnp.bfloat16), "hid", scatter_dimension=1, tiled=True
    ).astype(jnp.float32)
    mid_own = (tokens.astype(jnp.float32) + 0.5 * share).astype(jnp.bfloat16)
    return mid_own, lax.all_gather(mid_own, "hid", axis=1, tiled=True)


GROUP = ("bh", "bl")
VMEM = pl.BlockSpec(memory_space=pltpu.VMEM)
SMEM = pl.BlockSpec(memory_space=pltpu.SMEM)


def kernel_call(body, outs, ins, scratch=(), scalars=0, flops=0, moved=0, limit=40):
    return pl.pallas_call(
        body,
        out_shape=[jax.ShapeDtypeStruct(shape, dtype) for shape, dtype in outs],
        in_specs=[SMEM] * scalars + [VMEM] * (len(ins) - scalars),
        out_specs=[VMEM] * len(outs),
        scratch_shapes=list(scratch),
        compiler_params=pltpu.CompilerParams(vmem_limit_bytes=limit * 2**20),
        cost_estimate=pl.CostEstimate(flops=flops, bytes_accessed=moved, transcendentals=0),
    )(*ins)


def f32(values):
    return values.astype(jnp.float32)


def silu(values):
    return values / (1.0 + jnp.exp(-values))


def cut_kernel(*refs):
    *arrays, out_ref = refs
    parts, _, width = out_ref.shape
    for part in range(parts):
        at = 0
        for ref in arrays:
            rows = ref.shape[0]
            out_ref[part, at : at + rows, :] = ref[:, part * width : (part + 1) * width]
            at += rows


def part_kernel(both_ref, first_ref, second_ref):
    half, shard, _ = first_ref.shape
    skip = both_ref.shape[1] - shard
    first_ref[...] = both_ref[:half, skip:, :]
    second_ref[...] = both_ref[half:, skip:, :]


def norm_kernel(me_ref, whole_ref, gain_ref, near_ref, far_ref, out_ref, oth_ref):
    rows, width = near_ref.shape
    at = pl.ds(pl.multiple_of(me_ref[1] * rows, rows), rows)
    for place, ref in ((me_ref[2], near_ref), (1 - me_ref[2], far_ref)):
        ref[...] = whole_ref[at, pl.ds(pl.multiple_of(place * width, width), width)]
    oth = pl.ds(pl.multiple_of((1 - me_ref[1]) * rows, rows), rows)
    out_ref[...] = norm_rows(f32(whole_ref[at, :]), gain_ref[...]).astype(jnp.bfloat16)
    oth_ref[...] = norm_rows(f32(whole_ref[oth, :]), gain_ref[...]).astype(jnp.bfloat16)


def part_rows_kernel(ref, first_ref, second_ref):
    half = first_ref.shape[0]
    first_ref[...] = ref[:half]
    second_ref[...] = ref[half:]


def interleave(full_ref, base, block, own_refs, other_refs, me_l, last=False):
    for refs, turn in ((own_refs, me_l), (other_refs, 1 - me_l)):
        blocks = [(ref, j) for ref in refs for j in range(ref.shape[0])]
        for i, (ref, j) in enumerate(blocks):
            at = pl.multiple_of(base + (2 * i + turn) * block, block)
            skip = ref.shape[1] - block if last else 0
            full_ref[pl.ds(at, block), :] = ref[j, skip : skip + block, :]


def hidden_kernel(n_x, me_ref, *refs):
    pieces, (both_ref, both_x_ref, z_ref, zx_ref, h_ref, w_ref, x_ref) = refs[:n_x], refs[n_x:]
    me_l, me_a = me_ref[0], me_ref[2]
    part, block = w_ref.shape[0] // 2, z_ref.shape[1]
    interleave(w_ref, me_a * part, block, [both_ref], [both_x_ref], me_l)
    interleave(w_ref, (1 - me_a) * part, block, [z_ref], [zx_ref], me_l)
    at = 0
    for piece in pieces:
        x_ref[at : at + piece.shape[0], :] = piece[...]
        at += piece.shape[0]
    step = 256
    for at in range(0, x_ref.shape[0], step):
        pre = jnp.dot(x_ref[at : at + step, :], w_ref[...], preferred_element_type=jnp.float32)
        h_ref[at : at + step, :] = silu(pre).astype(jnp.bfloat16)


def sums_kernel(n_own, me_ref, own_ref, oth_ref, *refs):
    *blocks, kept_ref, sent_ref, w_ref = refs
    block = w_ref.shape[0] // 8
    interleave(w_ref, 0, block, blocks[:n_own], blocks[n_own:], me_ref[0], True)
    step = 256
    for h_ref, out_ref in ((oth_ref, sent_ref), (own_ref, kept_ref)):
        for at in range(0, h_ref.shape[0], step):
            out_ref[at : at + step, :] = lax.dot_general(
                h_ref[at : at + step, :],
                w_ref[...],
                (((1,), (1,)), ((), ())),
                preferred_element_type=jnp.float32,
            ).astype(out_ref.dtype)


def add_kernel(kept_ref, came_ref, *out_refs):
    rows = out_refs[0].shape[0]
    for k, out_ref in enumerate(out_refs):
        at = slice(k * rows, (k + 1) * rows)
        out_ref[...] = (kept_ref[at, :] + f32(came_ref[at, :])).astype(out_ref.dtype)


def mid_kernel(mine_ref, first_ref, *refs):
    *others, out_ref = refs
    total = first_ref[...]
    for other in others:
        total = total + f32(other[...])
    out_ref[...] = (f32(mine_ref[...]) + 0.5 * total).astype(jnp.bfloat16)


HALO = 16


def utter_kernel(first_ref, lengths_ref, out_ref, base_ref):
    position = first_ref[0] + lax.broadcasted_iota(jnp.int32, base_ref.shape, 0)

    def step(u, carry):
        end, utter = carry
        end = end + lengths_ref[u]
        return end, utter + jnp.where(position >= end, 1, 0)

    zero = jnp.zeros(base_ref.shape, jnp.int32)
    base_ref[...] = lax.fori_loop(0, lengths_ref.shape[0], step, (jnp.int32(0), zero))[1]
    for r in range(8):
        out_ref[r] = base_ref[1 + r : 1 + r + out_ref.shape[1], :]


def glu_kernel(
    me_ref, near_ref, near_oth_ref, far_ref, far_oth_ref, gain_ref, value_ref, gate_ref,
    glu_ref, head_ref, tail_ref, own_ref, mid_ref
):
    rows, width = near_ref.shape
    me_c, me_a = me_ref[1], me_ref[2]
    for core, near, far in ((me_c, near_ref, far_ref), (1 - me_c, near_oth_ref, far_oth_ref)):
        at = pl.ds(pl.multiple_of(core * rows, rows), rows)
        for place, ref in ((me_a, near), (1 - me_a, far)):
            mid_ref[at, pl.ds(pl.multiple_of(place * width, width), width)] = ref[...]
    own_ref[...] = mid_ref[:, pl.ds(pl.multiple_of(me_c * width, width), width)]
    normed = norm_rows(f32(mid_ref[...]), gain_ref[...]).astype(jnp.bfloat16)
    value = jnp.dot(normed, value_ref[...], preferred_element_type=jnp.float32)
    gate = jnp.dot(normed, gate_ref[...], preferred_element_type=jnp.float32)
    glu = (value / (1.0 + jnp.exp(-gate))).astype(jnp.bfloat16)
    glu_ref[...] = glu
    head_ref[...] = glu[:HALO]
    tail_ref[...] = glu[glu.shape[0] - HALO :]


def conv_rows(ext_ref, utter_ref, taps_ref, scale_ref, shift_ref, out_ref, tiles, step):
    width = out_ref.shape[1]
    taps = taps_ref.shape[0]
    lanes = 128
    group = 3 if width % (3 * lanes) == 0 else 1
    span = step + taps - 8

    def columns(i, _):
        at_lane = [pl.ds(pl.multiple_of((i * group + g) * lanes, lanes), lanes) for g in range(group)]
        for ext_at, at, out_at in tiles:
            centre = utter_ref[7, at + HALO - 8 : at + HALO - 8 + step, :]
            totals = [jnp.zeros((step, lanes), jnp.float32)] * group
            for r in range(8):
                cells = [ext_ref[ext_at + 1 + r : ext_at + 1 + r + span, c] for c in at_lane]
                for q in range(0, taps, 8):
                    same = utter_ref[r, at + q : at + q + step, :] == centre
                    for g, c in enumerate(at_lane):
                        term = cells[g][q : q + step] * taps_ref[q + r : q + r + 1, c]
                        totals[g] = totals[g] + jnp.where(same, term, 0.0)
            for total, c in zip(totals, at_lane):
                act = silu(total * scale_ref[:, c] + shift_ref[:, c])
                out_ref[out_at : out_at + step, c] = act.astype(out_ref.dtype)
        return 0

    lax.fori_loop(0, width // (group * lanes), columns, 0)


def inner_conv_kernel(glu_ref, utter_ref, taps_ref, scale_ref, shift_ref, out_ref, ext_ref):
    ext_ref[...] = f32(glu_ref[...])
    step = 2 * HALO
    tiles = [(at - HALO, at, at) for at in range(HALO, out_ref.shape[0] - HALO, step)]
    conv_rows(ext_ref, utter_ref, taps_ref, scale_ref, shift_ref, out_ref, tiles, step)


def edge_conv_kernel(
    act_ref, top_ref, glu_ref, bottom_ref, utter_ref, taps_ref, scale_ref, shift_ref, out_ref, ext_ref
):
    rows = out_ref.shape[0]
    last = rows - HALO
    out_ref[HALO:last, :] = act_ref[HALO:last, :]
    ext_ref[:HALO, :] = f32(top_ref[...])
    ext_ref[HALO : 3 * HALO, :] = f32(glu_ref[: 2 * HALO, :])
    ext_ref[3 * HALO : 5 * HALO, :] = f32(glu_ref[rows - 2 * HALO :, :])
    ext_ref[5 * HALO :, :] = f32(bottom_ref[...])
    tiles = [(0, 0, 0), (3 * HALO, last, last)]
    conv_rows(ext_ref, utter_ref, taps_ref, scale_ref, shift_ref, out_ref, tiles, HALO)


def utterances(rows, axis, lengths, taps):
    return kernel_call(
        utter_kernel,
        [((8, rows + taps - 8, 128), jnp.int32)],
        [(lax.axis_index(axis) * rows - HALO)[None], lengths],
        scratch=[pltpu.VMEM((rows + 2 * HALO, 128), jnp.int32)],
        scalars=2,
    )[0]


def grouped_conv_module(mid, me, axis, early, w_value, w_gate, depth_kernel, w_proj):
    half, width = mid[0].shape
    rows = 2 * half
    utter, conv_gain, bn_scale, bn_shift = early
    bf16 = jnp.bfloat16
    glu, head, tail, mid_own = kernel_call(
        glu_kernel,
        [((rows, width), bf16)] + [((HALO, width), bf16)] * 2 + [((rows, width), bf16)],
        [me, *mid, conv_gain, w_value, w_gate],
        scratch=[pltpu.VMEM((rows, 2 * width), bf16)],
        scalars=1,
        flops=4 * rows * w_value.size,
        moved=4 * w_value.size,
    )
    count = lax.axis_size(axis)
    top = lax.ppermute(tail, axis, [(i, i + 1) for i in range(count - 1)])
    bottom = lax.ppermute(head, axis, [(i + 1, i) for i in range(count - 1)])
    rest = [utter, depth_kernel, bn_scale, bn_shift]
    (act,) = kernel_call(
        inner_conv_kernel,
        [((rows, width), bf16)],
        [glu, *rest],
        scratch=[pltpu.VMEM((rows, width), jnp.float32)],
        flops=rows * depth_kernel.size,
        moved=16 * rows * width,
    )
    (act,) = kernel_call(
        edge_conv_kernel,
        [((rows, width), bf16)],
        [act, top, glu, bottom, *rest],
        scratch=[pltpu.VMEM((6 * HALO, width), jnp.float32)],
        flops=HALO * depth_kernel.size,
        moved=4 * rows * width,
    )
    act_full = lax.all_gather(act, "hid", axis=1, tiled=True)
    projected = jnp.dot(act_full, w_proj, preferred_element_type=jnp.float32)
    return (mid_own.astype(jnp.float32) + projected).astype(jnp.bfloat16)


def partner(values, step):
    return lax.ppermute(values, GROUP, [(i, i ^ step) for i in range(4)])


def swap(values, axis):
    return lax.ppermute(values, axis, SWAP)


def recut(parts):
    return lax.all_to_all(parts, GROUP, 0, 0)


def grouped_ffn(tokens, ffn_gain, w_in, w_out, early):
    rows, width = tokens.shape
    half = rows // 2
    shard, hid = w_in.shape
    wide = 2 * width
    units = hid // 4
    bf16 = jnp.bfloat16
    me_c = lax.axis_index("hid")
    me = jnp.stack([lax.axis_index("al"), me_c, lax.axis_index("ah")])
    tie = lax.optimization_barrier

    block, pair = (4, shard, units), (2, shard, units)
    in_far = swap(w_in, "ah")
    (both,) = kernel_call(cut_kernel, [((4, 2 * shard, units), bf16)], [w_in, w_out.T], limit=60)
    both = recut(both)
    whole = lax.all_gather(tokens, "hid", axis=1, tiled=True)
    *mine, normed, normed_oth = kernel_call(
        norm_kernel,
        [((half, width), bf16)] * 2 + [((half, wide), bf16)] * 2,
        [me, whole, ffn_gain[None, :]],
        scalars=1,
    )
    frames1 = partner(normed, 1)
    in_far, both, normed, normed_oth, frames1, early = tie(
        (in_far, both, normed, normed_oth, frames1, early)
    )
    both_x = swap(both, "al")
    (in_z,) = kernel_call(cut_kernel, [(block, bf16)], [in_far])
    in_z = recut(in_z)
    out_1, out_2 = kernel_call(part_kernel, [(pair, bf16)] * 2, [both])
    out_z1 = swap(out_1, "ah")
    frames2 = partner(normed, 2)
    frames1_oth = swap(frames1, "hid")
    both_x, in_z, out_z1, out_2, frames1_oth = tie((both_x, in_z, out_z1, out_2, frames1_oth))
    in_zx = swap(in_z, "al")
    out_z2 = swap(out_2, "ah")
    upper, lower = kernel_call(part_rows_kernel, [((half // 2, wide), bf16)] * 2, [frames2])
    frames3 = [partner(upper, 1), partner(lower, 1)]
    in_zx, out_z1, out_z2, frames3 = tie((in_zx, out_z1, out_z2, frames3))
    out_zx1 = swap(out_z1, "al")
    out_zx2 = swap(out_z2, "al")
    own = [normed, frames1, frames2, *frames3]
    others = [normed_oth, frames1_oth] + [swap(v, "hid") for v in own[2:]]

    def units_of(pieces):
        return kernel_call(
            functools.partial(hidden_kernel, len(pieces)),
            [((4 * half, units), bf16)],
            [me, *pieces, both, both_x, in_z, in_zx],
            scratch=[pltpu.VMEM((wide, units), bf16), pltpu.VMEM((4 * half, wide), bf16)],
            scalars=1,
        )[0]

    hidden = [units_of(own), units_of(others)]

    def products(own, other):
        return kernel_call(
            functools.partial(sums_kernel, len(own)),
            [((4 * half, width), jnp.float32), ((4 * half, width), bf16)],
            [me, *hidden, *own, *other],
            scratch=[pltpu.VMEM((width, units), bf16)],
            scalars=1,
        )

    def scatter(kept, sent):
        total = kernel_call(
            add_kernel,
            [((half, width), jnp.float32)] + [((half, width), bf16)] * 3,
            [kept, swap(sent, "hid")],
        )
        return [total[0]] + [partner(v, k + 1) for k, v in enumerate(total[1:])]

    near, out_zx1, out_zx2 = tie((products([both], [both_x]), out_zx1, out_zx2))
    far = products([out_z1, out_z2], [out_zx1, out_zx2])
    mine_near, mine_far = mine

    def mid(rows, parts):
        (own,) = kernel_call(mid_kernel, [((half, width), bf16)], [rows, *parts])
        return own, swap(own, "hid")

    near, parts = tie((mid(mine_near, scatter(*near)), scatter(*far)))
    return near + mid(mine_far, parts), me, early


def solution(mesh):
    n_tok, n_hid = mesh.shape["tok"], mesh.shape["hid"]
    grouped = n_tok == 16 and n_hid == 2
    if grouped:
        tok = ("ah", "bh", "bl", "al")
        inner = Mesh(mesh.devices.reshape(2, 2, 2, 2, n_hid), tok + ("hid",))
    else:
        tok, inner = "tok", mesh

    def local(tokens, ffn_gain, w_in, w_out, conv_gain, *rest):
        if grouped:
            w_value, w_gate, depth_kernel, bn_scale, bn_shift, w_proj, lengths = rest
            utter = utterances(tokens.shape[0], tok, lengths, depth_kernel.shape[0])
            early = utter, conv_gain[None, :], bn_scale[None, :], bn_shift[None, :]
            mid, me, early = grouped_ffn(tokens, ffn_gain, w_in, w_out, early)
            return grouped_conv_module(mid, me, tok, early, w_value, w_gate, depth_kernel, w_proj)
        mid_own, mid_full = gathered_ffn(tokens, ffn_gain, w_in, w_out)
        return conv_module(mid_own, mid_full, tok, conv_gain, *rest)

    placed = (
        P(tok, "hid"),
        P(),
        P(tok, "hid"),
        P("hid", tok),
        P(),
        P(None, "hid"),
        P(None, "hid"),
        P(None, "hid"),
        P("hid"),
        P("hid"),
        P(None, "hid"),
        P(),
    )
    return jax.shard_map(
        local, mesh=inner, in_specs=placed, out_specs=P(tok, "hid"), check_vma=False
    )
```

```python
import functools

import jax
import jax.numpy as jnp
from jax import lax
from jax.experimental import pallas as pl
from jax.experimental.pallas import tpu as pltpu
from jax.sharding import Mesh, PartitionSpec as P

SWAP = [(0, 1), (1, 0)]


def norm_rows(values, gain):
    mean = jnp.mean(values, axis=-1, keepdims=True)
    centred = values - mean
    var = jnp.mean(centred * centred, axis=-1, keepdims=True)
    return centred * lax.rsqrt(var + 1e-05) * gain


def padded(cells, axis, width):
    count = lax.axis_size(axis)
    ends = count - 1
    head = cells[:width]
    tail = cells[cells.shape[0] - width :]
    return jnp.concatenate(
        [
            lax.ppermute(tail, axis, [(i, (i + 1) % count) for i in range(ends)]),
            cells,
            lax.ppermute(head, axis, [((i + 1) % count, i) for i in range(ends)]),
        ],
        axis=0,
    )


def conv_module(mid_own, mid_full, axis, conv_gain, w_value, w_gate, depth_kernel, bn_scale, bn_shift, w_proj, lengths):
    rows, width = mid_own.shape
    mid_normed = norm_rows(mid_full.astype(jnp.float32), conv_gain).astype(jnp.bfloat16)
    value = jnp.dot(mid_normed, w_value, preferred_element_type=jnp.float32)
    gate = jnp.dot(mid_normed, w_gate, preferred_element_type=jnp.float32)
    glu = (value * jax.nn.sigmoid(gate)).astype(jnp.bfloat16)
    extended = padded(glu, axis, 16).astype(jnp.float32)
    ends = jnp.cumsum(lengths)
    first_row = lax.axis_index(axis) * rows - 16
    positions = first_row + jnp.arange(rows + 32, dtype=jnp.int32)
    utter = jnp.sum((ends[None, :] <= positions[:, None]).astype(jnp.int32), axis=1)
    centre = utter[16 : 16 + rows]
    conv = jnp.zeros((rows, width), jnp.float32)
    for tap in range(depth_kernel.shape[0]):
        same = (utter[tap + 1 : tap + 1 + rows] == centre)[:, None]
        conv = conv + jnp.where(
            same, extended[tap + 1 : tap + 1 + rows] * depth_kernel[tap][None, :], 0.0
        )
    act = jax.nn.silu(conv * bn_scale + bn_shift).astype(jnp.bfloat16)
    act_full = lax.all_gather(act, "hid", axis=1, tiled=True)
    projected = jnp.dot(act_full, w_proj, preferred_element_type=jnp.float32)
    return (mid_own.astype(jnp.float32) + projected).astype(jnp.bfloat16)


def gathered_ffn(tokens, ffn_gain, w_in, w_out):
    whole = lax.all_gather(tokens, "hid", axis=1, tiled=True)
    normed = norm_rows(whole.astype(jnp.float32), ffn_gain).astype(jnp.bfloat16)
    pre = jnp.dot(
        normed, lax.all_gather(w_in, "tok", axis=0, tiled=True), preferred_element_type=jnp.float32
    )
    hidden = jax.nn.silu(pre).astype(jnp.bfloat16)
    partial_sum = jnp.dot(
        hidden, lax.all_gather(w_out, "tok", axis=1, tiled=True), preferred_element_type=jnp.float32
    )
    share = lax.psum_scatter(
        partial_sum.astype(jnp.bfloat16), "hid", scatter_dimension=1, tiled=True
    ).astype(jnp.float32)
    mid_own = (tokens.astype(jnp.float32) + 0.5 * share).astype(jnp.bfloat16)
    return mid_own, lax.all_gather(mid_own, "hid", axis=1, tiled=True)


GROUP = ("bh", "bl")
VMEM = pl.BlockSpec(memory_space=pltpu.VMEM)
SMEM = pl.BlockSpec(memory_space=pltpu.SMEM)


def kernel_call(body, outs, ins, scratch=(), scalars=0, flops=0, moved=0, limit=40):
    return pl.pallas_call(
        body,
        out_shape=[jax.ShapeDtypeStruct(shape, dtype) for shape, dtype in outs],
        in_specs=[SMEM] * scalars + [VMEM] * (len(ins) - scalars),
        out_specs=[VMEM] * len(outs),
        scratch_shapes=list(scratch),
        compiler_params=pltpu.CompilerParams(vmem_limit_bytes=limit * 2**20),
        cost_estimate=pl.CostEstimate(flops=flops, bytes_accessed=moved, transcendentals=0),
    )(*ins)


def f32(values):
    return values.astype(jnp.float32)


def silu(values):
    return values / (1.0 + jnp.exp(-values))


def cut_kernel(*refs):
    *arrays, out_ref = refs
    parts, _, width = out_ref.shape
    for part in range(parts):
        at = 0
        for ref in arrays:
            rows = ref.shape[0]
            out_ref[part, at : at + rows, :] = ref[:, part * width : (part + 1) * width]
            at += rows


def part_kernel(both_ref, first_ref, second_ref):
    half, shard, _ = first_ref.shape
    skip = both_ref.shape[1] - shard
    first_ref[...] = both_ref[:half, skip:, :]
    second_ref[...] = both_ref[half:, skip:, :]


def norm_kernel(me_ref, whole_ref, gain_ref, near_ref, far_ref, out_ref, oth_ref):
    rows, width = near_ref.shape
    at = pl.ds(pl.multiple_of(me_ref[1] * rows, rows), rows)
    for place, ref in ((me_ref[2], near_ref), (1 - me_ref[2], far_ref)):
        ref[...] = whole_ref[at, pl.ds(pl.multiple_of(place * width, width), width)]
    oth = pl.ds(pl.multiple_of((1 - me_ref[1]) * rows, rows), rows)
    out_ref[...] = norm_rows(f32(whole_ref[at, :]), gain_ref[...]).astype(jnp.bfloat16)
    oth_ref[...] = norm_rows(f32(whole_ref[oth, :]), gain_ref[...]).astype(jnp.bfloat16)


def part_rows_kernel(ref, first_ref, second_ref):
    half = first_ref.shape[0]
    first_ref[...] = ref[:half]
    second_ref[...] = ref[half:]


def interleave(full_ref, base, block, own_refs, other_refs, me_l, last=False):
    for refs, turn in ((own_refs, me_l), (other_refs, 1 - me_l)):
        blocks = [(ref, j) for ref in refs for j in range(ref.shape[0])]
        for i, (ref, j) in enumerate(blocks):
            at = pl.multiple_of(base + (2 * i + turn) * block, block)
            skip = ref.shape[1] - block if last else 0
            full_ref[pl.ds(at, block), :] = ref[j, skip : skip + block, :]


def hidden_kernel(n_x, me_ref, *refs):
    pieces, (both_ref, both_x_ref, z_ref, zx_ref, h_ref, w_ref, x_ref) = refs[:n_x], refs[n_x:]
    me_l, me_a = me_ref[0], me_ref[2]
    part, block = w_ref.shape[0] // 2, z_ref.shape[1]
    interleave(w_ref, me_a * part, block, [both_ref], [both_x_ref], me_l)
    interleave(w_ref, (1 - me_a) * part, block, [z_ref], [zx_ref], me_l)
    at = 0
    for piece in pieces:
        x_ref[at : at + piece.shape[0], :] = piece[...]
        at += piece.shape[0]
    step = 256
    for at in range(0, x_ref.shape[0], step):
        pre = jnp.dot(x_ref[at : at + step, :], w_ref[...], preferred_element_type=jnp.float32)
        h_ref[at : at + step, :] = silu(pre).astype(jnp.bfloat16)


def sums_kernel(n_own, me_ref, own_ref, oth_ref, *refs):
    *blocks, kept_ref, sent_ref, w_ref = refs
    block = w_ref.shape[0] // 8
    interleave(w_ref, 0, block, blocks[:n_own], blocks[n_own:], me_ref[0], True)
    step = 256
    for h_ref, out_ref in ((oth_ref, sent_ref), (own_ref, kept_ref)):
        for at in range(0, h_ref.shape[0], step):
            out_ref[at : at + step, :] = lax.dot_general(
                h_ref[at : at + step, :],
                w_ref[...],
                (((1,), (1,)), ((), ())),
                preferred_element_type=jnp.float32,
            ).astype(out_ref.dtype)


def add_kernel(kept_ref, came_ref, *out_refs):
    rows = out_refs[0].shape[0]
    for k, out_ref in enumerate(out_refs):
        at = slice(k * rows, (k + 1) * rows)
        out_ref[...] = (kept_ref[at, :] + f32(came_ref[at, :])).astype(out_ref.dtype)


def mid_kernel(mine_ref, first_ref, *refs):
    *others, out_ref = refs
    total = first_ref[...]
    for other in others:
        total = total + f32(other[...])
    out_ref[...] = (f32(mine_ref[...]) + 0.5 * total).astype(jnp.bfloat16)


HALO = 16


def utter_kernel(first_ref, lengths_ref, out_ref, base_ref):
    position = first_ref[0] + lax.broadcasted_iota(jnp.int32, base_ref.shape, 0)

    def step(u, carry):
        end, utter = carry
        end = end + lengths_ref[u]
        return end, utter + jnp.where(position >= end, 1, 0)

    zero = jnp.zeros(base_ref.shape, jnp.int32)
    base_ref[...] = lax.fori_loop(0, lengths_ref.shape[0], step, (jnp.int32(0), zero))[1]
    for r in range(8):
        out_ref[r] = base_ref[1 + r : 1 + r + out_ref.shape[1], :]


def glu_kernel(
    me_ref, near_ref, near_oth_ref, far_ref, far_oth_ref, gain_ref, value_ref, gate_ref,
    glu_ref, head_ref, tail_ref, own_ref, mid_ref
):
    rows, width = near_ref.shape
    me_c, me_a = me_ref[1], me_ref[2]
    for core, near, far in ((me_c, near_ref, far_ref), (1 - me_c, near_oth_ref, far_oth_ref)):
        at = pl.ds(pl.multiple_of(core * rows, rows), rows)
        for place, ref in ((me_a, near), (1 - me_a, far)):
            mid_ref[at, pl.ds(pl.multiple_of(place * width, width), width)] = ref[...]
    own_ref[...] = mid_ref[:, pl.ds(pl.multiple_of(me_c * width, width), width)]
    normed = norm_rows(f32(mid_ref[...]), gain_ref[...]).astype(jnp.bfloat16)
    value = jnp.dot(normed, value_ref[...], preferred_element_type=jnp.float32)
    gate = jnp.dot(normed, gate_ref[...], preferred_element_type=jnp.float32)
    glu = (value / (1.0 + jnp.exp(-gate))).astype(jnp.bfloat16)
    glu_ref[...] = glu
    head_ref[...] = glu[:HALO]
    tail_ref[...] = glu[glu.shape[0] - HALO :]


def conv_rows(ext_ref, utter_ref, taps_ref, scale_ref, shift_ref, out_ref, tiles, step):
    width = out_ref.shape[1]
    taps = taps_ref.shape[0]
    lanes = 128
    group = 3 if width % (3 * lanes) == 0 else 1
    span = step + taps - 8

    def columns(i, _):
        at_lane = [pl.ds(pl.multiple_of((i * group + g) * lanes, lanes), lanes) for g in range(group)]
        for ext_at, at, out_at in tiles:
            centre = utter_ref[7, at + HALO - 8 : at + HALO - 8 + step, :]
            totals = [jnp.zeros((step, lanes), jnp.float32)] * group
            for r in range(8):
                cells = [ext_ref[ext_at + 1 + r : ext_at + 1 + r + span, c] for c in at_lane]
                for q in range(0, taps, 8):
                    same = utter_ref[r, at + q : at + q + step, :] == centre
                    for g, c in enumerate(at_lane):
                        term = cells[g][q : q + step] * taps_ref[q + r : q + r + 1, c]
                        totals[g] = totals[g] + jnp.where(same, term, 0.0)
            for total, c in zip(totals, at_lane):
                act = silu(total * scale_ref[:, c] + shift_ref[:, c])
                out_ref[out_at : out_at + step, c] = act.astype(out_ref.dtype)
        return 0

    lax.fori_loop(0, width // (group * lanes), columns, 0)


def inner_conv_kernel(glu_ref, utter_ref, taps_ref, scale_ref, shift_ref, out_ref, ext_ref):
    ext_ref[...] = f32(glu_ref[...])
    edge = jnp.zeros((HALO, out_ref.shape[1]), out_ref.dtype)
    out_ref[:HALO, :] = edge
    out_ref[out_ref.shape[0] - HALO :, :] = edge
    step = 2 * HALO
    tiles = [(at - HALO, at, at) for at in range(HALO, out_ref.shape[0] - HALO, step)]
    conv_rows(ext_ref, utter_ref, taps_ref, scale_ref, shift_ref, out_ref, tiles, step)


def edge_conv_kernel(
    top_ref, glu_ref, bottom_ref, utter_ref, taps_ref, scale_ref, shift_ref, out_ref, ext_ref
):
    rows = glu_ref.shape[0]
    last = rows - HALO
    ext_ref[:HALO, :] = f32(top_ref[...])
    ext_ref[HALO : 3 * HALO, :] = f32(glu_ref[: 2 * HALO, :])
    ext_ref[3 * HALO : 5 * HALO, :] = f32(glu_ref[rows - 2 * HALO :, :])
    ext_ref[5 * HALO :, :] = f32(bottom_ref[...])
    tiles = [(0, 0, 0), (3 * HALO, last, HALO)]
    conv_rows(ext_ref, utter_ref, taps_ref, scale_ref, shift_ref, out_ref, tiles, HALO)


def project_kernel(
    me_ref, inner_ref, inner_oth_ref, edge_ref, edge_oth_ref, mid_ref, w_ref, out_ref, act_ref
):
    rows, width = out_ref.shape
    last = rows - HALO
    me_c = me_ref[1]
    for core, inner, edge in (
        (me_c, inner_ref, edge_ref),
        (1 - me_c, inner_oth_ref, edge_oth_ref),
    ):
        at = pl.ds(pl.multiple_of(core * width, width), width)
        act_ref[:HALO, at] = edge[:HALO, :]
        act_ref[HALO:last, at] = inner[HALO:last, :]
        act_ref[last:, at] = edge[HALO:, :]
    projected = jnp.dot(act_ref[...], w_ref[...], preferred_element_type=jnp.float32)
    out_ref[...] = (f32(mid_ref[...]) + projected).astype(out_ref.dtype)


def utterances(rows, axis, lengths, taps):
    return kernel_call(
        utter_kernel,
        [((8, rows + taps - 8, 128), jnp.int32)],
        [(lax.axis_index(axis) * rows - HALO)[None], lengths],
        scratch=[pltpu.VMEM((rows + 2 * HALO, 128), jnp.int32)],
        scalars=2,
    )[0]


def grouped_conv_module(mid, me, axis, early, w_value, w_gate, depth_kernel, w_proj):
    half, width = mid[0].shape
    rows = 2 * half
    utter, conv_gain, bn_scale, bn_shift = early
    bf16 = jnp.bfloat16
    glu, head, tail, mid_own = kernel_call(
        glu_kernel,
        [((rows, width), bf16)] + [((HALO, width), bf16)] * 2 + [((rows, width), bf16)],
        [me, *mid, conv_gain, w_value, w_gate],
        scratch=[pltpu.VMEM((rows, 2 * width), bf16)],
        scalars=1,
        flops=4 * rows * w_value.size,
        moved=4 * w_value.size,
    )
    count = lax.axis_size(axis)
    top = lax.ppermute(tail, axis, [(i, i + 1) for i in range(count - 1)])
    bottom = lax.ppermute(head, axis, [(i + 1, i) for i in range(count - 1)])
    rest = [utter, depth_kernel, bn_scale, bn_shift]
    (inner,) = kernel_call(
        inner_conv_kernel,
        [((rows, width), bf16)],
        [glu, *rest],
        scratch=[pltpu.VMEM((rows, width), jnp.float32)],
        flops=rows * depth_kernel.size,
        moved=16 * rows * width,
    )
    inner_oth = swap(inner, "hid")
    (edge,) = kernel_call(
        edge_conv_kernel,
        [((2 * HALO, width), bf16)],
        [top, glu, bottom, *rest],
        scratch=[pltpu.VMEM((6 * HALO, width), jnp.float32)],
        flops=HALO * depth_kernel.size,
        moved=4 * rows * width,
    )
    (out,) = kernel_call(
        project_kernel,
        [((rows, width), bf16)],
        [me, inner, inner_oth, edge, swap(edge, "hid"), mid_own, w_proj],
        scratch=[pltpu.VMEM((rows, 2 * width), bf16)],
        scalars=1,
        flops=4 * rows * width * width,
        moved=2 * w_proj.size,
    )
    return out


def partner(values, step):
    return lax.ppermute(values, GROUP, [(i, i ^ step) for i in range(4)])


def swap(values, axis):
    return lax.ppermute(values, axis, SWAP)


def recut(parts):
    return lax.all_to_all(parts, GROUP, 0, 0)


def grouped_ffn(tokens, ffn_gain, w_in, w_out, early):
    rows, width = tokens.shape
    half = rows // 2
    shard, hid = w_in.shape
    wide = 2 * width
    units = hid // 4
    bf16 = jnp.bfloat16
    me_c = lax.axis_index("hid")
    me = jnp.stack([lax.axis_index("al"), me_c, lax.axis_index("ah")])
    tie = lax.optimization_barrier

    block, pair = (4, shard, units), (2, shard, units)
    in_far = swap(w_in, "ah")
    (both,) = kernel_call(cut_kernel, [((4, 2 * shard, units), bf16)], [w_in, w_out.T], limit=60)
    both = recut(both)
    whole = lax.all_gather(tokens, "hid", axis=1, tiled=True)
    *mine, normed, normed_oth = kernel_call(
        norm_kernel,
        [((half, width), bf16)] * 2 + [((half, wide), bf16)] * 2,
        [me, whole, ffn_gain[None, :]],
        scalars=1,
    )
    frames1 = partner(normed, 1)
    in_far, both, normed, normed_oth, frames1, early = tie(
        (in_far, both, normed, normed_oth, frames1, early)
    )
    both_x = swap(both, "al")
    (in_z,) = kernel_call(cut_kernel, [(block, bf16)], [in_far])
    in_z = recut(in_z)
    out_1, out_2 = kernel_call(part_kernel, [(pair, bf16)] * 2, [both])
    out_z1 = swap(out_1, "ah")
    frames2 = partner(normed, 2)
    frames1_oth = swap(frames1, "hid")
    both_x, in_z, out_z1, out_2, frames1_oth = tie((both_x, in_z, out_z1, out_2, frames1_oth))
    in_zx = swap(in_z, "al")
    out_z2 = swap(out_2, "ah")
    upper, lower = kernel_call(part_rows_kernel, [((half // 2, wide), bf16)] * 2, [frames2])
    frames3 = [partner(upper, 1), partner(lower, 1)]
    in_zx, out_z1, out_z2, frames3 = tie((in_zx, out_z1, out_z2, frames3))
    out_zx1 = swap(out_z1, "al")
    out_zx2 = swap(out_z2, "al")
    own = [normed, frames1, frames2, *frames3]
    others = [normed_oth, frames1_oth] + [swap(v, "hid") for v in own[2:]]

    def units_of(pieces):
        return kernel_call(
            functools.partial(hidden_kernel, len(pieces)),
            [((4 * half, units), bf16)],
            [me, *pieces, both, both_x, in_z, in_zx],
            scratch=[pltpu.VMEM((wide, units), bf16), pltpu.VMEM((4 * half, wide), bf16)],
            scalars=1,
        )[0]

    hidden = [units_of(own), units_of(others)]

    def products(own, other):
        return kernel_call(
            functools.partial(sums_kernel, len(own)),
            [((4 * half, width), jnp.float32), ((4 * half, width), bf16)],
            [me, *hidden, *own, *other],
            scratch=[pltpu.VMEM((width, units), bf16)],
            scalars=1,
        )

    def scatter(kept, sent):
        total = kernel_call(
            add_kernel,
            [((half, width), jnp.float32)] + [((half, width), bf16)] * 3,
            [kept, swap(sent, "hid")],
        )
        return [total[0]] + [partner(v, k + 1) for k, v in enumerate(total[1:])]

    near, out_zx1, out_zx2 = tie((products([both], [both_x]), out_zx1, out_zx2))
    far = products([out_z1, out_z2], [out_zx1, out_zx2])
    mine_near, mine_far = mine

    def mid(rows, parts):
        (own,) = kernel_call(mid_kernel, [((half, width), bf16)], [rows, *parts])
        return own, swap(own, "hid")

    near, parts = tie((mid(mine_near, scatter(*near)), scatter(*far)))
    return near + mid(mine_far, parts), me, early


def solution(mesh):
    n_tok, n_hid = mesh.shape["tok"], mesh.shape["hid"]
    grouped = n_tok == 16 and n_hid == 2
    if grouped:
        tok = ("ah", "bh", "bl", "al")
        inner = Mesh(mesh.devices.reshape(2, 2, 2, 2, n_hid), tok + ("hid",))
    else:
        tok, inner = "tok", mesh

    def local(tokens, ffn_gain, w_in, w_out, conv_gain, *rest):
        if grouped:
            w_value, w_gate, depth_kernel, bn_scale, bn_shift, w_proj, lengths = rest
            utter = utterances(tokens.shape[0], tok, lengths, depth_kernel.shape[0])
            early = utter, conv_gain[None, :], bn_scale[None, :], bn_shift[None, :]
            mid, me, early = grouped_ffn(tokens, ffn_gain, w_in, w_out, early)
            return grouped_conv_module(mid, me, tok, early, w_value, w_gate, depth_kernel, w_proj)
        mid_own, mid_full = gathered_ffn(tokens, ffn_gain, w_in, w_out)
        return conv_module(mid_own, mid_full, tok, conv_gain, *rest)

    placed = (
        P(tok, "hid"),
        P(),
        P(tok, "hid"),
        P("hid", tok),
        P(),
        P(None, "hid"),
        P(None, "hid"),
        P(None, "hid"),
        P("hid"),
        P("hid"),
        P(None, "hid"),
        P(),
    )
    return jax.shard_map(
        local, mesh=inner, in_specs=placed, out_specs=P(tok, "hid"), check_vma=False
    )
```
